32 devices in a mesh: seq: 8 (over z, y), head: 4 (over x, core).
Axes of the slice: x: 2, y: 2, z: 4, core: 2. Of those that a mesh axis runs over, the one named last changes fastest.
Arguments:
- queries: bfloat16 [4096, 8192], P(('seq', 'head')), may hold values from -18 to 18
- keys: bfloat16 [4096, 1024], P(('seq', 'head')), may hold values from -6 to 6
- values: bfloat16 [4096, 1024], P(('seq', 'head')), may hold values from -6 to 6
- upstream: bfloat16 [4096, 8192], P(('seq', 'head')), may hold values from -96 to 96
- send_rows: int32 [8, 768], P('seq'), may hold values from -1 to 511, as said below
- recv_rows: int32 [8, 512], P('seq'), may hold values from 0 to 767, as said below
- doc_lengths: int32 [8, 4], P('seq'), may hold values from 1 to 256, 512 in all within a row
- pair_docs: int32 [32], replicated, may hold values from 0 to 31, each once
- response_mask: int32 [4096], P('seq'), may hold values 0 or 1
- policy_logp: float32 [4096], P('seq'), may hold values from -2.5 to -0.05
- ref_logp: float32 [4096], P('seq'), may hold values from -2.5 to -0.05
Outputs:
- grad_queries: bfloat16 [4096, 8192], P(('seq', 'head'))
- key_row_gradient: bfloat16 [4096, 1024], P(('seq', 'head'))
- value_row_gradient: bfloat16 [4096, 1024], P(('seq', 'head'))
The draws below stay inside these ranges and needn't reach their ends.
Inputs may be any that keep to these rules, and one draw needn't show every extreme that they name: `send_rows`: entry o * 96 + k of loader group s names the row (of its 512) that owner group o takes as its k-th row from s, or -1 for an empty slot. Every row of a loader group is named exactly once; in each block of 96 entries the named rows come first; every loader group fills some block completely. `recv_rows`: entry p of owner group o names the received slot s * 96 + k (k-th slot from loader group s) that holds its row p. The named slots of an owner group are distinct and are exactly the filled ones. `doc_lengths`: row o lists the lengths of owner group o's 4 dialogues in the order in which they fill its 512 rows; each row sums to 512. Dialogue j of owner group o has the number o * 4 + j. Pair k is the chosen dialogue pair_docs[2k] and the rejected dialogue pair_docs[2k+1]. `response_mask`: 1 marks a response token.
All inputs are finite; a program needn't handle non-finite values. No bound on the sum of `response_mask` on one device may be relied on, other than what follows from the above.
Results may differ from the reference program's by a relative error of at most 0.0088.
Values may be sent and summed in bfloat16 or wider, within the bound.
A program may use at most 128 MiB of HBM per device.

```python
import math
import jax
import jax.numpy as jnp
import numpy as np
from jax import lax

QUERY_HEAD_COUNT = 64
KEY_VALUE_HEADS = 8
HEAD_SIZE = 128
DOC_OWN = 4
GROUP_TOKEN_ROWS = 512
TOKEN_TOTAL = 4096
CAP = 96
DOCS = 32
N_SEQ = 8


def routing_tables(key):
    base = jax.random.fold_in(key, 7001)
    divided_keys = jax.random.split(base, 6)
    groups = TOKEN_TOTAL // GROUP_TOKEN_ROWS
    average = GROUP_TOKEN_ROWS // groups
    spread = average // 2
    capacity = average + spread
    halfway = groups // 2
    delta = jax.random.randint(divided_keys[0], (halfway,), -spread, spread + 1).astype(jnp.int32)
    delta = delta.at[0].set(spread)
    fills = jnp.concatenate([average + delta, average - delta]).astype(jnp.int32)
    fills = jax.random.permutation(divided_keys[1], fills)
    rotate_owner = jax.random.permutation(divided_keys[2], groups).astype(jnp.int32)
    rotate_loader = jax.random.permutation(divided_keys[3], groups).astype(jnp.int32)
    counts = fills[(rotate_owner[None, :] - rotate_loader[:, None]) % groups]
    loader_order = jax.vmap(lambda sub: jax.random.permutation(sub, groups))(jax.random.split(divided_keys[4], groups)).astype(jnp.int32)
    ordered = jnp.take_along_axis(counts, loader_order, axis=1)
    before = jnp.cumsum(ordered, axis=1) - ordered
    loader_index = jnp.arange(groups, dtype=jnp.int32)
    starts = jnp.zeros((groups, groups), jnp.int32).at[loader_index[:, None], loader_order].set(before)
    offset = jnp.arange(capacity, dtype=jnp.int32)
    send_table = jnp.where(offset[None, None, :] < counts[:, :, None], starts[:, :, None] + offset[None, None, :], -1)
    send_table = send_table.reshape(groups, groups * capacity).astype(jnp.int32)
    owner_order = jax.vmap(lambda sub: jax.random.permutation(sub, groups))(jax.random.split(divided_keys[5], groups)).astype(jnp.int32)
    run_length = jnp.take_along_axis(counts.T, owner_order, axis=1)
    run_end = jnp.cumsum(run_length, axis=1)
    position = jnp.arange(GROUP_TOKEN_ROWS, dtype=jnp.int32)
    which_run = jnp.sum((position[None, :, None] >= run_end[:, None, :]).astype(jnp.int32), axis=2)
    source = jnp.take_along_axis(owner_order, which_run, axis=1)
    run_start = jnp.take_along_axis(run_end - run_length, which_run, axis=1)
    recv_table = (source * capacity + position[None, :] - run_start).astype(jnp.int32)
    return (send_table, recv_table)


def draw_send_rows(key, part):
    return routing_tables(key)[0]


def draw_recv_rows(key, part):
    return routing_tables(key)[1]


def attention_inputs(key):
    base = jax.random.fold_in(key, 9103)
    divided_keys = jax.random.split(base, 3)
    rows_of_key = jnp.clip(jax.random.normal(divided_keys[0], (TOKEN_TOTAL, KEY_VALUE_HEADS * HEAD_SIZE), jnp.float32), -6.0, 6.0)
    query_rows = jnp.clip(jax.random.normal(divided_keys[2], (TOKEN_TOTAL, QUERY_HEAD_COUNT * HEAD_SIZE), jnp.float32), -6.0, 6.0)
    return (query_rows, rows_of_key)


def draw_queries(key, part):
    return attention_inputs(key)[0].astype(jnp.bfloat16)


def draw_keys(key, part):
    return attention_inputs(key)[1].astype(jnp.bfloat16)


def plant(values, stream_key, least, top_value):
    longest = values.shape.index(max(values.shape))
    spots = []
    for shift in (0, 1):
        where = [jax.random.randint(jax.random.fold_in(stream_key, axis), (), 0, length) for axis, length in enumerate(values.shape)]
        where[longest] = (where[longest] + shift) % values.shape[longest]
        spots.append(tuple(where))
    return values.at[spots[0]].set(least).at[spots[1]].set(top_value)


def levels(stream_key, shape, cuts, low, top_value):
    level, own = 1.0, jax.random.fold_in(stream_key, 6)
    for dim, parts in cuts:
        steps = jnp.exp(jax.random.uniform(jax.random.fold_in(own, dim), (parts,), jnp.float32, low / len(cuts), top_value / len(cuts)))
        level = level * jnp.repeat(steps, shape[dim] // parts).reshape([-1 if axis == dim else 1 for axis in range(len(shape))])
    return level


def profile(count, total, limit, slope):
    portions = [(1 << 20) // math.isqrt(rank ** slope) + 1 for rank in range(2, count + 1)]
    surplus, holding = total - limit - (count - 1), [1] * (count - 1)
    while surplus > 0:
        free = [i for i in range(count - 1) if holding[i] < limit]
        pool, left = sum([portions[i] for i in free]), surplus
        for i in free:
            addition = min(limit - holding[i], max(1, left * portions[i] // pool), surplus)
            holding[i] = holding[i] + addition
            surplus = surplus - addition
    return np.array([limit] + holding)


def uneven(own_key, count, total, reach, slope):
    if count == 2:
        one = jax.random.randint(own_key, (), max(1, total - reach), min(reach, total - 1) + 1)
        return jnp.stack([one, total - one])
    tallies = jnp.asarray(profile(count, total, reach, slope), jnp.int32)
    couples = (count - 1) // 2
    donor, sink = tallies[1:1 + 2 * couples:2], tallies[2:2 + 2 * couples:2]
    room = jnp.minimum(donor - 1, reach - sink)
    passed = jax.random.randint(jax.random.fold_in(own_key, 1), (couples,), 0, 1 << 20) % (room + 1)
    tallies = tallies.at[1:1 + 2 * couples:2].set(donor - passed).at[2:2 + 2 * couples:2].set(sink + passed)
    return tallies[jax.random.permutation(jax.random.fold_in(own_key, 2), count)]


def scatter_about(stream_key, extent, scale, reach, cuts=(), kind=jnp.bfloat16):
    entries = jax.random.normal(stream_key, extent, jnp.float32) * scale
    if len(cuts) > 0:
        entries = levels(stream_key, extent, cuts, -0.22, 0.18) * entries
    return jnp.clip(entries, min=-reach, max=reach).astype(kind)


def setup_inputs(seed: int = 0) -> dict:
    splits = jax.random.split(jax.random.key(seed), 12)
    return {
        "queries": draw_queries(jax.random.fold_in(splits[11], 71), 0),
        "keys": draw_keys(jax.random.fold_in(splits[11], 71), 0),
        "values": scatter_about(splits[2], (TOKEN_TOTAL, KEY_VALUE_HEADS * HEAD_SIZE), 1.0, 6.0, ((0, 32),)),
        "upstream": scatter_about(splits[3], (TOKEN_TOTAL, QUERY_HEAD_COUNT * HEAD_SIZE), 16.0, 96.0, ((0, 32),)),
        "send_rows": draw_send_rows(jax.random.fold_in(splits[11], 71), 0),
        "recv_rows": draw_recv_rows(jax.random.fold_in(splits[11], 71), 0),
        "doc_lengths": jax.vmap(lambda own: uneven(own, DOC_OWN, GROUP_TOKEN_ROWS, GROUP_TOKEN_ROWS // 2, 2))(jax.random.split(splits[6], N_SEQ)).reshape((N_SEQ, DOC_OWN)).astype(jnp.int32),
        "pair_docs": jax.random.permutation(splits[7], DOCS).astype(jnp.int32),
        "response_mask": plant((jax.random.randint(splits[8], (TOKEN_TOTAL,), 0, 4) < 3).astype(jnp.int32), jax.random.fold_in(splits[8], 1), 0, 1),
        "policy_logp": jnp.clip(-2.5 + 2.45 * jax.random.uniform(splits[9], (TOKEN_TOTAL,), jnp.float32) ** levels(splits[9], (TOKEN_TOTAL,), ((0, 8),), -0.2, 0.2), -2.5, -0.05),
        "ref_logp": jnp.clip(-2.5 + 2.45 * jax.random.uniform(splits[10], (TOKEN_TOTAL,), jnp.float32) ** levels(splits[10], (TOKEN_TOTAL,), ((0, 8),), -0.2, 0.2), -2.5, -0.05),
    }


dpo_beta = 0.1

def head_grads(query_block, key_block, value_block, grad_block, allowed, score_scale):
    scores = lax.dot_general(query_block, key_block, (((1,), (1,)), ((), ())), preferred_element_type=jnp.float32) * score_scale
    scores = jnp.where(allowed, scores, -1e+30)
    highest = lax.optimization_barrier(jnp.max(scores, axis=1, keepdims=True))
    lifted = jnp.exp(scores - highest)
    probs = lifted / lax.optimization_barrier(jnp.sum(lifted, axis=1, keepdims=True))
    probs_low = probs.astype(jnp.bfloat16)
    output = jnp.dot(probs_low, value_block, preferred_element_type=jnp.float32)
    row_dot = lax.optimization_barrier(jnp.sum(grad_block.astype(jnp.float32) * output, axis=1, keepdims=True))
    value_gradient = lax.dot_general(probs_low, grad_block, (((0,), (0,)), ((), ())), preferred_element_type=jnp.float32)
    grad_probs = lax.dot_general(grad_block, value_block, (((1,), (1,)), ((), ())), preferred_element_type=jnp.float32)
    grad_scores = (probs * (grad_probs - row_dot) * score_scale).astype(jnp.bfloat16)
    grad_query = jnp.dot(grad_scores, key_block, preferred_element_type=jnp.float32).astype(jnp.bfloat16)
    key_gradient = lax.dot_general(grad_scores, query_block, (((0,), (0,)), ((), ())), preferred_element_type=jnp.float32)
    return (grad_query, key_gradient, value_gradient)

def reference(queries, keys, values, upstream, send_rows, recv_rows, doc_lengths, pair_docs, response_mask, policy_logp, ref_logp):
    owners = jnp.arange(N_SEQ, dtype=jnp.int32)
    source = (recv_rows // CAP).astype(jnp.int32)
    within = (recv_rows % CAP).astype(jnp.int32)
    group_row = send_rows[source, owners[:, None] * CAP + within]
    loader_row = (source * GROUP_TOKEN_ROWS + group_row).astype(jnp.int32)
    position = jnp.arange(GROUP_TOKEN_ROWS, dtype=jnp.int32)
    doc_ends = jnp.cumsum(doc_lengths, axis=1).astype(jnp.int32)
    doc_of_row = lax.optimization_barrier(jnp.sum((position[None, :, None] >= doc_ends[:, None, :]).astype(jnp.int32), axis=2)).astype(jnp.int32)
    token_gap = (response_mask.astype(jnp.float32) * (policy_logp - ref_logp)).reshape(N_SEQ, GROUP_TOKEN_ROWS)
    member = doc_of_row[:, :, None] == jnp.arange(DOC_OWN, dtype=jnp.int32)[None, None, :]
    doc_gap = lax.optimization_barrier(jnp.sum(jnp.where(member, token_gap[:, :, None], 0.0), axis=1)).reshape(DOCS)
    chosen_docs = pair_docs[0::2]
    rejected_docs = pair_docs[1::2]
    margin = dpo_beta * (doc_gap[chosen_docs] - doc_gap[rejected_docs])
    pair_weight = dpo_beta * jax.nn.sigmoid(-margin)
    doc_coef = jnp.zeros((DOCS,), jnp.float32).at[chosen_docs].set(-pair_weight).at[rejected_docs].set(pair_weight)
    row_coef = jnp.take_along_axis(doc_coef.reshape(N_SEQ, DOC_OWN), doc_of_row, axis=1)
    group_share = QUERY_HEAD_COUNT // KEY_VALUE_HEADS
    score_scale = 1.0 / math.sqrt(HEAD_SIZE)

    def one_group(items):
        rows, coef_rows, docs = items
        query_rows = jnp.take(queries, rows, axis=0)
        rows_of_key = jnp.take(keys, rows, axis=0)
        rows_of_value = jnp.take(values, rows, axis=0)
        grad_out = (coef_rows[:, None] * jnp.take(upstream, rows, axis=0).astype(jnp.float32)).astype(jnp.bfloat16)
        allowed = (docs[:, None] == docs[None, :]) & (position[None, :] <= position[:, None])
        query_heads = query_rows.reshape(GROUP_TOKEN_ROWS, QUERY_HEAD_COUNT, HEAD_SIZE).transpose(1, 0, 2)
        grad_heads = grad_out.reshape(GROUP_TOKEN_ROWS, QUERY_HEAD_COUNT, HEAD_SIZE).transpose(1, 0, 2)
        heads_of_key = rows_of_key.reshape(GROUP_TOKEN_ROWS, KEY_VALUE_HEADS, HEAD_SIZE).transpose(1, 0, 2)
        heads_of_value = rows_of_value.reshape(GROUP_TOKEN_ROWS, KEY_VALUE_HEADS, HEAD_SIZE).transpose(1, 0, 2)

        def one_head(pieces):
            query_block, grad_block, head_index = pieces
            shared = head_index // group_share
            return head_grads(query_block, heads_of_key[shared], heads_of_value[shared], grad_block, allowed, score_scale)
        grad_query, key_gradient, value_gradient = lax.map(one_head, (query_heads, grad_heads, jnp.arange(QUERY_HEAD_COUNT, dtype=jnp.int32)))
        grad_query = grad_query.transpose(1, 0, 2).reshape(GROUP_TOKEN_ROWS, QUERY_HEAD_COUNT * HEAD_SIZE)
        key_gradient = key_gradient.reshape(KEY_VALUE_HEADS, group_share, GROUP_TOKEN_ROWS, HEAD_SIZE).sum(axis=1).astype(jnp.bfloat16)
        value_gradient = value_gradient.reshape(KEY_VALUE_HEADS, group_share, GROUP_TOKEN_ROWS, HEAD_SIZE).sum(axis=1).astype(jnp.bfloat16)
        key_gradient = key_gradient.transpose(1, 0, 2).reshape(GROUP_TOKEN_ROWS, KEY_VALUE_HEADS * HEAD_SIZE)
        value_gradient = value_gradient.transpose(1, 0, 2).reshape(GROUP_TOKEN_ROWS, KEY_VALUE_HEADS * HEAD_SIZE)
        return (grad_query, key_gradient, value_gradient)
    owner_query, key_at_owner, value_at_owner = lax.map(one_group, (loader_row, row_coef, doc_of_row))
    flattened_rows = loader_row.reshape(TOKEN_TOTAL)
    grad_queries = jnp.zeros((TOKEN_TOTAL, QUERY_HEAD_COUNT * HEAD_SIZE), jnp.bfloat16).at[flattened_rows].set(owner_query.reshape(TOKEN_TOTAL, QUERY_HEAD_COUNT * HEAD_SIZE))
    key_row_gradient = jnp.zeros((TOKEN_TOTAL, KEY_VALUE_HEADS * HEAD_SIZE), jnp.bfloat16).at[flattened_rows].set(key_at_owner.reshape(TOKEN_TOTAL, KEY_VALUE_HEADS * HEAD_SIZE))
    value_row_gradient = jnp.zeros((TOKEN_TOTAL, KEY_VALUE_HEADS * HEAD_SIZE), jnp.bfloat16).at[flattened_rows].set(value_at_owner.reshape(TOKEN_TOTAL, KEY_VALUE_HEADS * HEAD_SIZE))
    return (grad_queries, key_row_gradient, value_row_gradient)
```

```python
import functools
import math

import jax
import jax.numpy as jnp
from jax import lax
from jax.experimental import pallas as pl
from jax.experimental.pallas import tpu as pltpu
from jax.sharding import PartitionSpec as P

HEAD_SIZE = 128
DPO_BETA = 0.1
F32 = jnp.float32
BF16 = jnp.bfloat16
VMEM_BYTES = 56 * 1024 * 1024

ROWS_ROWS = (((1,), (1,)), ((), ()))
COLS_COLS = (((0,), (0,)), ((), ()))


def matmul(left, right, dims=(((1,), (0,)), ((), ()))):
    return lax.dot_general(left, right, dims, preferred_element_type=F32)


def attention_kernel(
    cap,
    per_shared,
    kv_here,
    row_info_ref,
    send_cols_ref,
    send_row_ref,
    query_ref,
    upstream_ref,
    kv_ref,
    grad_query_ref,
    grad_kv_ref,
    grad_slots,
):
    owner = pl.program_id(0)
    owners = pl.num_programs(0)
    group_rows = query_ref.shape[0]
    sources = kv_ref.shape[0]
    slot_count = sources * cap
    kv_columns = kv_ref.shape[-1]
    info = row_info_ref[0]
    recv_row = info[0:1, :]
    local_row = info[1:2, :]
    start_row = info[2:3, :]
    coef_row = info[3:4, :]

    slot_iota = lax.broadcasted_iota(jnp.int32, (slot_count, group_rows), 0).astype(F32)
    slot_to_row = jnp.where(slot_iota == recv_row, 1.0, 0.0).astype(BF16)
    slots = kv_ref[...].reshape(slot_count, kv_columns)
    kv_own = matmul(slot_to_row, slots, COLS_COLS).astype(BF16)

    send_column = jnp.transpose(send_cols_ref[0])[:cap, 0:1]
    lane = lax.broadcasted_iota(jnp.int32, (cap, group_rows), 1).astype(F32)
    pick = jnp.where(lane == send_column, 1.0, 0.0).astype(BF16)
    query_slots = matmul(pick, query_ref[...]).astype(BF16)
    upstream_slots = matmul(pick, upstream_ref[...])

    slot = lax.broadcasted_iota(jnp.int32, (cap, group_rows), 0).astype(F32)
    mine = slot == local_row
    position = jnp.sum(jnp.where(mine, lane, 0.0), axis=1, keepdims=True)
    start = jnp.sum(jnp.where(mine, start_row, 0.0), axis=1, keepdims=True)
    coef = jnp.sum(jnp.where(mine, coef_row, 0.0), axis=1, keepdims=True)
    grad_out = (coef * upstream_slots).astype(BF16)
    allowed = (lane >= start) & (lane <= position)

    score_scale = 1.0 / math.sqrt(HEAD_SIZE)
    exp_scale = score_scale * math.log2(math.e)
    grad_kv = []
    grad_query = []
    for shared in range(kv_here):
        key_block = kv_own[:, 2 * shared * HEAD_SIZE : (2 * shared + 1) * HEAD_SIZE]
        value_block = kv_own[:, (2 * shared + 1) * HEAD_SIZE : (2 * shared + 2) * HEAD_SIZE]
        probs_parts, score_parts, query_parts, out_parts = [], [], [], []
        for member in range(per_shared):
            head = shared * per_shared + member
            columns = slice(head * HEAD_SIZE, (head + 1) * HEAD_SIZE)
            query_block = query_slots[:, columns]
            grad_block = grad_out[:, columns]
            scores = jnp.where(allowed, matmul(query_block, key_block, ROWS_ROWS), -1e30)
            highest = jnp.max(scores, axis=1, keepdims=True)
            lifted = jnp.exp2((scores - highest) * exp_scale)
            probs = lifted * (1.0 / jnp.sum(lifted, axis=1, keepdims=True))
            probs_low = probs.astype(BF16)
            grad_probs = matmul(grad_block, value_block, ROWS_ROWS)
            row_dot = jnp.sum(probs_low.astype(F32) * grad_probs, axis=1, keepdims=True)
            grad_scores = (probs * ((grad_probs - row_dot) * score_scale)).astype(BF16)
            probs_parts.append(probs_low)
            score_parts.append(grad_scores)
            query_parts.append(query_block)
            out_parts.append(grad_block)
        grad_scores = jnp.concatenate(score_parts, axis=0)
        head_query = matmul(grad_scores, key_block).astype(BF16)
        for member in range(per_shared):
            grad_query.append(head_query[member * cap : (member + 1) * cap])
        grad_kv.append(matmul(grad_scores, jnp.concatenate(query_parts, axis=0), COLS_COLS))
        grad_kv.append(
            matmul(
                jnp.concatenate(probs_parts, axis=0), jnp.concatenate(out_parts, axis=0), COLS_COLS
            )
        )
    grad_slots[pl.ds(pl.multiple_of(owner * cap, 16), cap), :] = jnp.concatenate(grad_query, axis=1)
    grad_own = jnp.concatenate(grad_kv, axis=1).astype(BF16)
    grad_kv_ref[...] = (
        matmul(slot_to_row, grad_own).astype(BF16).reshape(grad_kv_ref.shape)
    )

    @pl.when(owner == owners - 1)
    def _():
        row = lax.broadcasted_iota(jnp.int32, (group_rows, slot_count), 0).astype(F32)
        place = jnp.where(row == send_row_ref[0:1, :], 1.0, 0.0).astype(BF16)
        grad_query_ref[...] = matmul(place, grad_slots[...]).astype(BF16)


def attention(cap, per_shared, kv_here, row_info, send_cols, send_row, query, upstream, kv_slots):
    owners = row_info.shape[0]
    group_rows, columns = query.shape
    slot_count = owners * cap
    kv_columns = kv_slots.shape[-1]
    whole = lambda array: pl.BlockSpec(array.shape, lambda i: (0,) * array.ndim)
    kv_spec = pl.BlockSpec((owners, None, cap, kv_columns), lambda i: (0, i, 0, 0))
    return pl.pallas_call(
        functools.partial(attention_kernel, cap, per_shared, kv_here),
        grid=(owners,),
        in_specs=[
            pl.BlockSpec((1,) + row_info.shape[1:], lambda i: (i, 0, 0)),
            pl.BlockSpec((1,) + send_cols.shape[1:], lambda i: (i, 0, 0)),
            whole(send_row),
            whole(query),
            whole(upstream),
            kv_spec,
        ],
        out_specs=[whole(query), kv_spec],
        out_shape=[
            jax.ShapeDtypeStruct(query.shape, BF16),
            jax.ShapeDtypeStruct(kv_slots.shape, BF16),
        ],
        scratch_shapes=[pltpu.VMEM((slot_count, columns), BF16)],
        compiler_params=pltpu.CompilerParams(vmem_limit_bytes=VMEM_BYTES),
        name="attention_grads",
    )(row_info, send_cols, send_row, query, upstream, kv_slots)


def pair_coefficients(doc_gap, pair_docs):
    docs = jnp.arange(doc_gap.shape[0], dtype=jnp.int32)
    chosen = pair_docs[0::2][:, None] == docs[None, :]
    rejected = pair_docs[1::2][:, None] == docs[None, :]
    sign = chosen.astype(F32) - rejected.astype(F32)
    margin = DPO_BETA * jnp.sum(sign * doc_gap[None, :], axis=1)
    weight = DPO_BETA * jax.nn.sigmoid(-margin)
    return -jnp.sum(sign * weight[:, None], axis=0)


def body(
    queries,
    keys,
    values,
    upstream,
    send_rows,
    recv_rows,
    doc_lengths,
    pair_docs,
    response_mask,
    policy_logp,
    ref_logp,
):
    tok_rows = queries.shape[0]
    head_devices = lax.axis_size("head")
    owners = lax.axis_size("seq")
    group_rows = tok_rows * head_devices
    slot_count = send_rows.shape[1]
    cap = slot_count // owners
    kv_heads = keys.shape[1] // HEAD_SIZE
    kv_here = kv_heads // head_devices
    per_shared = queries.shape[1] // keys.shape[1]

    kv = jnp.stack(
        [keys.reshape(tok_rows, kv_heads, HEAD_SIZE), values.reshape(tok_rows, kv_heads, HEAD_SIZE)],
        axis=2,
    ).reshape(tok_rows, 2 * kv_heads * HEAD_SIZE)
    kv_group = lax.all_to_all(kv, "head", split_axis=1, concat_axis=0, tiled=True)

    doc_len = doc_lengths[0]
    doc_count = doc_len.shape[0]
    doc_ends = jnp.cumsum(doc_len)
    position = jnp.arange(group_rows, dtype=jnp.int32)
    doc_of_row = jnp.sum((position[:, None] >= doc_ends[None, :]).astype(jnp.int32), axis=1)
    member = doc_of_row[:, None] == jnp.arange(doc_count, dtype=jnp.int32)[None, :]
    token_gap = response_mask.astype(F32) * (policy_logp - ref_logp)
    doc_gap = jnp.sum(jnp.where(member, token_gap[:, None], 0.0), axis=0)
    facts = jnp.concatenate(
        [send_rows[0].astype(F32), recv_rows[0].astype(F32), doc_len.astype(F32), doc_gap]
    )
    facts = jnp.pad(facts, (0, -facts.shape[0] % 128))
    facts = lax.all_gather(facts, "seq", axis=0)

    kv_all = lax.all_gather(kv_group, "seq", axis=0)
    query_group = lax.all_to_all(queries, "head", split_axis=1, concat_axis=0, tiled=True)
    upstream_group = lax.all_to_all(upstream, "head", split_axis=1, concat_axis=0, tiled=True)

    send_all = facts[:, :slot_count]
    recv_all = facts[:, slot_count : slot_count + group_rows]
    at = slot_count + group_rows
    len_all = facts[:, at : at + doc_count]
    gap_all = facts[:, at + doc_count : at + 2 * doc_count]
    doc_coef = pair_coefficients(gap_all.reshape(-1), pair_docs).reshape(owners, doc_count)
    ends = jnp.cumsum(len_all, axis=1)
    starts = ends - len_all
    place = jnp.arange(group_rows, dtype=jnp.int32).astype(F32)
    inside = (place[None, :, None] >= starts[:, None, :]) & (place[None, :, None] < ends[:, None, :])
    start_of_row = jnp.sum(jnp.where(inside, starts[:, None, :], 0.0), axis=2)
    coef_of_row = jnp.sum(jnp.where(inside, doc_coef[:, None, :], 0.0), axis=2)
    first_slot = (lax.axis_index("seq") * cap).astype(F32)
    zero = jnp.zeros_like(recv_all)
    row_info = jnp.stack(
        [recv_all, recv_all - first_slot, start_of_row, coef_of_row, zero, zero, zero, zero], axis=1
    )
    own_send = send_rows[0].astype(F32)
    send_cols = jnp.pad(
        own_send.reshape(owners, 1, cap), ((0, 0), (0, 7), (0, -cap % 128)), constant_values=-1.0
    )
    send_row = jnp.broadcast_to(own_send[None, :], (8, slot_count))

    row = jnp.arange(group_rows, dtype=jnp.int32).astype(F32)
    slot_of_row = (send_all[:, :, None] == row[None, None, :]).astype(BF16)
    kv_slots = jnp.einsum("sjr,src->sjc", slot_of_row, kv_all, preferred_element_type=F32)
    kv_slots = kv_slots.astype(BF16).reshape(owners, owners, cap, -1)

    grad_query, grad_slots = attention(
        cap,
        per_shared,
        kv_here,
        row_info,
        send_cols,
        send_row,
        query_group,
        upstream_group,
        kv_slots,
    )

    grad_slots = grad_slots.reshape(owners, slot_count, -1)
    grad_kv = jnp.einsum("sjr,sjc->src", slot_of_row, grad_slots, preferred_element_type=F32)
    grad_kv = grad_kv.astype(BF16)
    grad_kv = lax.psum_scatter(grad_kv, "seq", scatter_dimension=0, tiled=True)[0]
    final_query = lax.all_to_all(grad_query, "head", split_axis=0, concat_axis=1, tiled=True)
    final_kv = lax.all_to_all(grad_kv, "head", split_axis=0, concat_axis=1, tiled=True)
    final_kv = final_kv.reshape(tok_rows, kv_heads, 2, HEAD_SIZE)
    return (
        final_query,
        final_kv[:, :, 0].reshape(tok_rows, -1),
        final_kv[:, :, 1].reshape(tok_rows, -1),
    )


def solution(mesh):
    rows = P(("seq", "head"), None)
    return jax.shard_map(
        body,
        mesh=mesh,
        in_specs=(
            rows,
            rows,
            rows,
            rows,
            P("seq", None),
            P("seq", None),
            P("seq", None),
            P(),
            P("seq"),
            P("seq"),
            P("seq"),
        ),
        out_specs=(rows, rows, rows),
        check_vma=False,
    )
```

```python
import functools
import math

import jax
import jax.numpy as jnp
from jax import lax
from jax.experimental import pallas as pl
from jax.experimental.pallas import tpu as pltpu
from jax.sharding import PartitionSpec as P

HEAD_SIZE = 128
DPO_BETA = 0.1
F32 = jnp.float32
BF16 = jnp.bfloat16
VMEM_BYTES = 56 * 1024 * 1024

ROWS_ROWS = (((1,), (1,)), ((), ()))
COLS_COLS = (((0,), (0,)), ((), ()))


def matmul(left, right, dims=(((1,), (0,)), ((), ()))):
    return lax.dot_general(left, right, dims, preferred_element_type=F32)


def attention_kernel(
    cap,
    per_shared,
    kv_here,
    row_info_ref,
    send_cols_ref,
    send_row_ref,
    query_ref,
    upstream_ref,
    kv_ref,
    grad_query_ref,
    grad_kv_ref,
    grad_slots,
):
    owner = pl.program_id(0)
    owners = pl.num_programs(0)
    group_rows = query_ref.shape[0]
    sources = kv_ref.shape[0]
    slot_count = sources * cap
    kv_columns = kv_ref.shape[-1]
    info = row_info_ref[0]
    recv_row = info[0:1, :]
    local_row = info[1:2, :]
    start_row = info[2:3, :]
    coef_row = info[3:4, :]

    slot_iota = lax.broadcasted_iota(jnp.int32, (slot_count, group_rows), 0).astype(F32)
    slot_to_row = jnp.where(slot_iota == recv_row, 1.0, 0.0).astype(BF16)
    slots = kv_ref[...].reshape(slot_count, kv_columns)
    kv_own = matmul(slot_to_row, slots, COLS_COLS).astype(BF16)

    send_column = jnp.transpose(send_cols_ref[0])[:cap, 0:1]
    lane = lax.broadcasted_iota(jnp.int32, (cap, group_rows), 1).astype(F32)
    pick = jnp.where(lane == send_column, 1.0, 0.0).astype(BF16)
    query_slots = matmul(pick, query_ref[...]).astype(BF16)
    upstream_slots = matmul(pick, upstream_ref[...])

    slot = lax.broadcasted_iota(jnp.int32, (cap, group_rows), 0).astype(F32)
    mine = slot == local_row
    position = jnp.sum(jnp.where(mine, lane, 0.0), axis=1, keepdims=True)
    start = jnp.sum(jnp.where(mine, start_row, 0.0), axis=1, keepdims=True)
    coef = jnp.sum(jnp.where(mine, coef_row, 0.0), axis=1, keepdims=True)
    grad_out = (coef * upstream_slots).astype(BF16)
    allowed = (lane >= start) & (lane <= position)

    score_scale = 1.0 / math.sqrt(HEAD_SIZE)
    exp_scale = score_scale * math.log2(math.e)
    grad_key, grad_value = [], []
    grad_query = []
    for shared in range(kv_here):
        key_block = kv_own[:, shared * HEAD_SIZE : (shared + 1) * HEAD_SIZE]
        value_at = (kv_here + shared) * HEAD_SIZE
        value_block = kv_own[:, value_at : value_at + HEAD_SIZE]
        probs_parts, score_parts, query_parts, out_parts = [], [], [], []
        for member in range(per_shared):
            head = shared * per_shared + member
            columns = slice(head * HEAD_SIZE, (head + 1) * HEAD_SIZE)
            query_block = query_slots[:, columns]
            grad_block = grad_out[:, columns]
            scores = jnp.where(allowed, matmul(query_block, key_block, ROWS_ROWS), -1e30)
            highest = jnp.max(scores, axis=1, keepdims=True)
            lifted = jnp.exp2((scores - highest) * exp_scale)
            probs = lifted * (1.0 / jnp.sum(lifted, axis=1, keepdims=True))
            probs_low = probs.astype(BF16)
            grad_probs = matmul(grad_block, value_block, ROWS_ROWS)
            row_dot = jnp.sum(probs_low.astype(F32) * grad_probs, axis=1, keepdims=True)
            grad_scores = (probs * ((grad_probs - row_dot) * score_scale)).astype(BF16)
            probs_parts.append(probs_low)
            score_parts.append(grad_scores)
            query_parts.append(query_block)
            out_parts.append(grad_block)
        grad_scores = jnp.concatenate(score_parts, axis=0)
        head_query = matmul(grad_scores, key_block).astype(BF16)
        for member in range(per_shared):
            grad_query.append(head_query[member * cap : (member + 1) * cap])
        grad_key.append(matmul(grad_scores, jnp.concatenate(query_parts, axis=0), COLS_COLS))
        grad_value.append(
            matmul(
                jnp.concatenate(probs_parts, axis=0), jnp.concatenate(out_parts, axis=0), COLS_COLS
            )
        )
    grad_slots[pl.ds(pl.multiple_of(owner * cap, 16), cap), :] = jnp.concatenate(grad_query, axis=1)
    grad_own = jnp.concatenate(grad_key + grad_value, axis=1).astype(BF16)
    grad_kv_ref[...] = (
        matmul(slot_to_row, grad_own).astype(BF16).reshape(grad_kv_ref.shape)
    )

    @pl.when(owner == owners - 1)
    def _():
        row = lax.broadcasted_iota(jnp.int32, (group_rows, slot_count), 0).astype(F32)
        place = jnp.where(row == send_row_ref[0:1, :], 1.0, 0.0).astype(BF16)
        grad_query_ref[...] = matmul(place, grad_slots[...]).astype(BF16)


def attention(cap, per_shared, kv_here, row_info, send_cols, send_row, query, upstream, kv_slots):
    owners = row_info.shape[0]
    group_rows, columns = query.shape
    slot_count = owners * cap
    kv_columns = kv_slots.shape[-1]
    whole = lambda array: pl.BlockSpec(array.shape, lambda i: (0,) * array.ndim)
    kv_spec = pl.BlockSpec((owners, None, cap, kv_columns), lambda i: (0, i, 0, 0))
    return pl.pallas_call(
        functools.partial(attention_kernel, cap, per_shared, kv_here),
        grid=(owners,),
        in_specs=[
            pl.BlockSpec((1,) + row_info.shape[1:], lambda i: (i, 0, 0)),
            pl.BlockSpec((1,) + send_cols.shape[1:], lambda i: (i, 0, 0)),
            whole(send_row),
            whole(query),
            whole(upstream),
            kv_spec,
        ],
        out_specs=[whole(query), kv_spec],
        out_shape=[
            jax.ShapeDtypeStruct(query.shape, BF16),
            jax.ShapeDtypeStruct(kv_slots.shape, BF16),
        ],
        scratch_shapes=[pltpu.VMEM((slot_count, columns), BF16)],
        compiler_params=pltpu.CompilerParams(vmem_limit_bytes=VMEM_BYTES),
        name="attention_grads",
    )(row_info, send_cols, send_row, query, upstream, kv_slots)


def mesh_place():
    return lax.axis_index("seq"), lax.axis_index("head")


def ring_place(index, size):
    half = size // 2
    up, side = index // 2, index % 2
    return up + side * (2 * half - 1 - 2 * up)


def ring_index(place, size):
    half = size // 2
    side = place // half
    up = place + side * (2 * half - 1 - 2 * place)
    return up * 2 + side


def remote(src, dst, send_sem, recv_sem, seq, head):
    return pltpu.make_async_remote_copy(
        src_ref=src,
        dst_ref=dst,
        send_sem=send_sem,
        recv_sem=recv_sem,
        device_id=(seq, head),
        device_id_type=pl.DeviceIdType.MESH,
    )


def greet(seq, head, seq_peers, heads):
    barrier = pltpu.get_barrier_semaphore()
    for peer in seq_peers:
        pl.semaphore_signal(
            barrier, inc=1, device_id=(peer, head), device_id_type=pl.DeviceIdType.MESH
        )
    for away in range(1, heads):
        pl.semaphore_signal(
            barrier,
            inc=1,
            device_id=(seq, lax.rem(head + away, heads)),
            device_id_type=pl.DeviceIdType.MESH,
        )
    pl.semaphore_wait(barrier, len(seq_peers) + heads - 1)


def gather_kernel(
    owners,
    heads,
    query_in,
    upstream_in,
    key_in,
    value_in,
    facts_in,
    query_out,
    upstream_out,
    kv_out,
    facts_out,
    local_sem,
    head_send,
    head_recv,
    facts_send,
    facts_recv,
    ring_send,
    ring_recv,
):
    seq, head = mesh_place()
    tok = query_in.shape[0]
    wide = query_out.shape[1]
    narrow = kv_out.shape[2] // 2
    group_rows = kv_out.shape[1]
    greet(seq, head, [lax.rem(seq + away, owners) for away in range(1, owners)], heads)

    rows = pl.ds(pl.multiple_of(head * tok, tok), tok)

    def columns(peer, width):
        return pl.ds(pl.multiple_of(peer * width, width), width)

    items = [
        (key_in, kv_out.at[seq, rows, pl.ds(0, narrow)], narrow),
        (value_in, kv_out.at[seq, rows, pl.ds(narrow, narrow)], narrow),
        (query_in, query_out.at[rows], wide),
        (upstream_in, upstream_out.at[rows], wide),
    ]
    locals_, sends = [], []
    for item, (src, dst, width) in enumerate(items):
        copy = pltpu.make_async_copy(src.at[:, columns(head, width)], dst, local_sem.at[item])
        copy.start()
        locals_.append(copy)
        for away in range(1, heads):
            peer = lax.rem(head + away, heads)
            copy = remote(
                src.at[:, columns(peer, width)],
                dst,
                head_send.at[item, away - 1],
                head_recv.at[item, away - 1],
                seq,
                peer,
            )
            copy.start()
            sends.append((item, copy))
    fact_copy = pltpu.make_async_copy(facts_in, facts_out.at[seq], local_sem.at[len(items)])
    fact_copy.start()
    fact_sends = []
    for away in range(1, owners):
        copy = remote(
            facts_in,
            facts_out.at[seq],
            facts_send.at[away - 1],
            facts_recv.at[away - 1],
            lax.rem(seq + away, owners),
            head,
        )
        copy.start()
        fact_sends.append(copy)

    locals_[0].wait()
    locals_[1].wait()
    for item, copy in sends:
        if item < 2:
            copy.wait_recv()

    place = ring_place(seq, owners)
    right = ring_index(lax.rem(place + 1, owners), owners)
    left = ring_index(lax.rem(place + owners - 1, owners), owners)
    part = group_rows // 2
    full = (owners - 1) // 2
    last = {}
    ring = []
    for step in range(owners // 2):
        for chunk in range(2):
            for way in range(2):
                if step == full and chunk != way:
                    continue
                if step > 0:
                    last.pop((way, chunk)).wait_recv()
                if way == 0:
                    shard = ring_index(lax.rem(place + owners - step, owners), owners)
                else:
                    shard = ring_index(lax.rem(place + step, owners), owners)
                block = kv_out.at[shard, pl.ds(chunk * part, part)]
                copy = remote(
                    block,
                    block,
                    ring_send.at[way, step, chunk],
                    ring_recv.at[way, step, chunk],
                    right if way == 0 else left,
                    head,
                )
                copy.start()
                last[(way, chunk)] = copy
                ring.append(copy)
    for copy in last.values():
        copy.wait_recv()
    for item, copy in sends:
        if item >= 2:
            copy.wait_recv()
    for copy in fact_sends:
        copy.wait_recv()
    locals_[2].wait()
    locals_[3].wait()
    fact_copy.wait()
    for copy in [c for _, c in sends] + fact_sends + ring:
        copy.wait_send()


def gather(owners, heads, queries, upstream, keys, values, facts):
    tok = queries.shape[0]
    group_rows = tok * heads
    group = jax.ShapeDtypeStruct((group_rows, queries.shape[1] // heads), BF16)
    kv = jax.ShapeDtypeStruct((owners, group_rows, 2 * keys.shape[1] // heads), BF16)
    dma = pltpu.SemaphoreType.DMA
    anywhere = pl.BlockSpec(memory_space=pl.ANY)
    return pl.pallas_call(
        functools.partial(gather_kernel, owners, heads),
        in_specs=[anywhere] * 5,
        out_specs=[anywhere] * 4,
        out_shape=[group, group, kv, jax.ShapeDtypeStruct((owners,) + facts.shape, F32)],
        scratch_shapes=[
            dma((5,)),
            dma((4, heads - 1)),
            dma((4, heads - 1)),
            dma((owners - 1,)),
            dma((owners - 1,)),
            dma((2, owners // 2, 2)),
            dma((2, owners // 2, 2)),
        ],
        compiler_params=pltpu.CompilerParams(
            collective_id=0, has_side_effects=True, vmem_limit_bytes=VMEM_BYTES
        ),
        name="gather_rows",
    )(queries, upstream, keys, values, facts)


def scatter_kernel(
    owners,
    heads,
    send_ref,
    slots_ref,
    query_in,
    query_out,
    key_out,
    value_out,
    sums,
    final,
    local_sem,
    head_send,
    head_recv,
    ring_send,
    ring_recv,
):
    seq, head = mesh_place()
    tok = query_out.shape[0]
    wide = query_in.shape[1]
    group_rows = query_in.shape[0]
    narrow = slots_ref.shape[2] // 2
    slot_count = slots_ref.shape[1]
    part = group_rows // 2
    place = ring_place(seq, owners)
    right = ring_index(lax.rem(place + 1, owners), owners)
    left = ring_index(lax.rem(place + owners - 1, owners), owners)
    greet(seq, head, [right, left], heads)

    def rows_of(peer):
        return pl.ds(pl.multiple_of(peer * tok, tok), tok)

    def exchange(item, src, dst, width):
        mine = dst.at[:, pl.ds(pl.multiple_of(head * width, width), width)]
        local = pltpu.make_async_copy(src.at[rows_of(head)], mine, local_sem.at[item])
        local.start()
        sends = []
        for away in range(1, heads):
            peer = lax.rem(head + away, heads)
            copy = remote(
                src.at[rows_of(peer)],
                mine,
                head_send.at[item, away - 1],
                head_recv.at[item, away - 1],
                seq,
                peer,
            )
            copy.start()
            sends.append(copy)
        return local, sends

    moved = [exchange(0, query_in, query_out, wide)]

    def shard_of(way, step):
        if way == 0:
            return ring_index(lax.rem(place + 2 * owners - 1 - step, owners), owners)
        return ring_index(lax.rem(place + 1 + step, owners), owners)

    def partial_sum(way, step, chunk):
        shard = shard_of(way, step)
        row = lax.broadcasted_iota(jnp.int32, (part, slot_count), 0).astype(F32) + float(chunk * part)
        spread = jnp.where(row == send_ref[shard], 1.0, 0.0).astype(BF16)
        return matmul(spread, slots_ref[shard, :, way * narrow : (way + 1) * narrow])

    def hop(way, step, chunk):
        return remote(
            sums.at[way, step, chunk],
            sums.at[way, step + 1, chunk],
            ring_send.at[way, step, chunk],
            ring_recv.at[way, step, chunk],
            right if way == 0 else left,
            head,
        )

    every = [(way, chunk) for chunk in range(2) for way in range(2)]
    for way, chunk in every:
        sums[way, 0, chunk] = partial_sum(way, 0, chunk).astype(BF16)
        hop(way, 0, chunk).start()

    def one_step(step, carry):
        for way, chunk in every:
            own = partial_sum(way, step, chunk)
            hop(way, step - 1, chunk).wait_recv()
            sums[way, step, chunk] = (own + sums[way, step, chunk].astype(F32)).astype(BF16)
            hop(way, step, chunk).start()
        return carry

    lax.fori_loop(1, owners - 1, one_step, 0)
    for way in range(2):
        for chunk in range(2):
            own = partial_sum(way, owners - 1, chunk)
            hop(way, owners - 2, chunk).wait_recv()
            total = own + sums[way, owners - 1, chunk].astype(F32)
            final[way, chunk * part : (chunk + 1) * part] = total.astype(BF16)
        moved.append(exchange(1 + way, final.at[way], key_out if way == 0 else value_out, narrow))

    def drain(step, carry):
        for way, chunk in every:
            hop(way, step, chunk).wait_send()
        return carry

    lax.fori_loop(0, owners - 1, drain, 0)
    for local, sends in moved:
        local.wait()
        for copy in sends:
            copy.wait()


def scatter(owners, heads, send_all, grad_slots, grad_query):
    group_rows, wide = grad_query.shape
    narrow = grad_slots.shape[2] // 2
    tok = group_rows // heads
    dma = pltpu.SemaphoreType.DMA
    anywhere = pl.BlockSpec(memory_space=pl.ANY)
    vmem = pl.BlockSpec(memory_space=pltpu.VMEM)
    return pl.pallas_call(
        functools.partial(scatter_kernel, owners, heads),
        in_specs=[vmem, vmem, anywhere],
        out_specs=[anywhere] * 3,
        out_shape=[
            jax.ShapeDtypeStruct((tok, wide * heads), BF16),
            jax.ShapeDtypeStruct((tok, narrow * heads), BF16),
            jax.ShapeDtypeStruct((tok, narrow * heads), BF16),
        ],
        scratch_shapes=[
            pltpu.VMEM((2, owners, 2, group_rows // 2, narrow), BF16),
            pltpu.VMEM((2, group_rows, narrow), BF16),
            dma((3,)),
            dma((3, heads - 1)),
            dma((3, heads - 1)),
            dma((2, owners - 1, 2)),
            dma((2, owners - 1, 2)),
        ],
        compiler_params=pltpu.CompilerParams(
            collective_id=1, has_side_effects=True, vmem_limit_bytes=VMEM_BYTES
        ),
        name="scatter_grads",
    )(send_all, grad_slots, grad_query)


def pair_coefficients(doc_gap, pair_docs):
    docs = jnp.arange(doc_gap.shape[0], dtype=jnp.int32)
    chosen = pair_docs[0::2][:, None] == docs[None, :]
    rejected = pair_docs[1::2][:, None] == docs[None, :]
    sign = chosen.astype(F32) - rejected.astype(F32)
    margin = DPO_BETA * jnp.sum(sign * doc_gap[None, :], axis=1)
    weight = DPO_BETA * jax.nn.sigmoid(-margin)
    return -jnp.sum(sign * weight[:, None], axis=0)


def body(
    queries,
    keys,
    values,
    upstream,
    send_rows,
    recv_rows,
    doc_lengths,
    pair_docs,
    response_mask,
    policy_logp,
    ref_logp,
):
    tok_rows = queries.shape[0]
    head_devices = lax.axis_size("head")
    owners = lax.axis_size("seq")
    group_rows = tok_rows * head_devices
    slot_count = send_rows.shape[1]
    cap = slot_count // owners
    kv_heads = keys.shape[1] // HEAD_SIZE
    kv_here = kv_heads // head_devices
    per_shared = queries.shape[1] // keys.shape[1]

    doc_len = doc_lengths[0]
    doc_count = doc_len.shape[0]
    doc_ends = jnp.cumsum(doc_len)
    position = jnp.arange(group_rows, dtype=jnp.int32)
    doc_of_row = jnp.sum((position[:, None] >= doc_ends[None, :]).astype(jnp.int32), axis=1)
    member = doc_of_row[:, None] == jnp.arange(doc_count, dtype=jnp.int32)[None, :]
    token_gap = response_mask.astype(F32) * (policy_logp - ref_logp)
    doc_gap = jnp.sum(jnp.where(member, token_gap[:, None], 0.0), axis=0)
    facts = jnp.concatenate(
        [send_rows[0].astype(F32), recv_rows[0].astype(F32), doc_len.astype(F32), doc_gap]
    )
    facts = jnp.pad(facts, (0, -facts.shape[0] % 1024)).reshape(-1, 128)
    query_group, upstream_group, kv_all, facts = gather(
        owners, head_devices, queries, upstream, keys, values, facts
    )
    facts = facts.reshape(owners, -1)

    send_all = facts[:, :slot_count]
    recv_all = facts[:, slot_count : slot_count + group_rows]
    at = slot_count + group_rows
    len_all = facts[:, at : at + doc_count]
    gap_all = facts[:, at + doc_count : at + 2 * doc_count]
    doc_coef = pair_coefficients(gap_all.reshape(-1), pair_docs).reshape(owners, doc_count)
    ends = jnp.cumsum(len_all, axis=1)
    starts = ends - len_all
    place = jnp.arange(group_rows, dtype=jnp.int32).astype(F32)
    inside = (place[None, :, None] >= starts[:, None, :]) & (place[None, :, None] < ends[:, None, :])
    start_of_row = jnp.sum(jnp.where(inside, starts[:, None, :], 0.0), axis=2)
    coef_of_row = jnp.sum(jnp.where(inside, doc_coef[:, None, :], 0.0), axis=2)
    first_slot = (lax.axis_index("seq") * cap).astype(F32)
    zero = jnp.zeros_like(recv_all)
    row_info = jnp.stack(
        [recv_all, recv_all - first_slot, start_of_row, coef_of_row, zero, zero, zero, zero], axis=1
    )
    own_send = send_rows[0].astype(F32)
    send_cols = jnp.pad(
        own_send.reshape(owners, 1, cap), ((0, 0), (0, 7), (0, -cap % 128)), constant_values=-1.0
    )
    send_row = jnp.broadcast_to(own_send[None, :], (8, slot_count))

    row = jnp.arange(group_rows, dtype=jnp.int32).astype(F32)
    slot_of_row = (send_all[:, :, None] == row[None, None, :]).astype(BF16)
    kv_slots = jnp.einsum("sjr,src->sjc", slot_of_row, kv_all, preferred_element_type=F32)
    kv_slots = kv_slots.astype(BF16).reshape(owners, owners, cap, -1)

    grad_query, grad_slots = attention(
        cap,
        per_shared,
        kv_here,
        row_info,
        send_cols,
        send_row,
        query_group,
        upstream_group,
        kv_slots,
    )

    grad_slots = grad_slots.reshape(owners, slot_count, -1)
    return tuple(
        scatter(owners, head_devices, send_all[:, None, :], grad_slots, grad_query)
    )


def solution(mesh):
    rows = P(("seq", "head"), None)
    return jax.shard_map(
        body,
        mesh=mesh,
        in_specs=(
            rows,
            rows,
            rows,
            rows,
            P("seq", None),
            P("seq", None),
            P("seq", None),
            P(),
            P("seq"),
            P("seq"),
            P("seq"),
        ),
        out_specs=(rows, rows, rows),
        check_vma=False,
    )
```

```python
import functools
import math

import jax
import jax.numpy as jnp
from jax import lax
from jax.experimental import pallas as pl
from jax.experimental.pallas import tpu as pltpu
from jax.sharding import PartitionSpec as P

HEAD_SIZE = 128
DPO_BETA = 0.1
F32 = jnp.float32
BF16 = jnp.bfloat16
VMEM_BYTES = 56 * 1024 * 1024

ROWS_ROWS = (((1,), (1,)), ((), ()))
COLS_COLS = (((0,), (0,)), ((), ()))


def matmul(left, right, dims=(((1,), (0,)), ((), ()))):
    return lax.dot_general(left, right, dims, preferred_element_type=F32)


def attention_kernel(
    cap,
    per_shared,
    kv_here,
    row_info_ref,
    send_cols_ref,
    send_row_ref,
    query_ref,
    upstream_ref,
    kv_ref,
    grad_query_ref,
    grad_kv_ref,
    grad_slots,
):
    owner = pl.program_id(0)
    owners = pl.num_programs(0)
    group_rows = query_ref.shape[0]
    sources = kv_ref.shape[0]
    slot_count = sources * cap
    kv_columns = kv_ref.shape[-1]
    info = row_info_ref[0]
    recv_row = info[0:1, :]
    local_row = info[1:2, :]
    coef_row = info[3:4, :]

    columns_of = jnp.transpose(info)
    recv_column = columns_of[:, 0:1]
    local_column = columns_of[:, 1:2]
    start_column = columns_of[:, 2:3]

    slot_lane = lax.broadcasted_iota(jnp.int32, (group_rows, slot_count), 1).astype(F32)
    row_to_slot = jnp.where(slot_lane == recv_column, 1.0, 0.0).astype(BF16)
    slots = kv_ref[...].reshape(slot_count, kv_columns)
    kv_own = matmul(row_to_slot, slots).astype(BF16)

    send_column = jnp.transpose(send_cols_ref[0])[:cap, 0:1]
    lane = lax.broadcasted_iota(jnp.int32, (cap, group_rows), 1).astype(F32)
    pick = jnp.where(lane == send_column, 1.0, 0.0).astype(BF16)
    query_slots = matmul(pick, query_ref[...]).astype(BF16)
    upstream_slots = matmul(pick, upstream_ref[...])
    slot = lax.broadcasted_iota(jnp.int32, (cap, group_rows), 0).astype(F32)
    coef = jnp.sum(jnp.where(slot == local_row, coef_row, 0.0), axis=1, keepdims=True)
    grad_out = (coef * upstream_slots).astype(BF16)

    across = lax.broadcasted_iota(jnp.int32, (group_rows, cap), 1).astype(F32)
    down = lax.broadcasted_iota(jnp.int32, (group_rows, cap), 0).astype(F32)
    mine = across == local_column
    position = jnp.sum(jnp.where(mine, down, 0.0), axis=0, keepdims=True)
    start = jnp.sum(jnp.where(mine, start_column, 0.0), axis=0, keepdims=True)
    stacked = per_shared * cap
    position = jnp.concatenate([position] * per_shared, axis=1)
    start = jnp.concatenate([start] * per_shared, axis=1)
    key_row = lax.broadcasted_iota(jnp.int32, (group_rows, stacked), 0).astype(F32)
    bias = jnp.where((key_row >= start) & (key_row <= position), 0.0, -1e30)

    score_scale = 1.0 / math.sqrt(HEAD_SIZE)
    exp_scale = score_scale * math.log2(math.e)
    width = next((w for w in (256, 128) if stacked % w == 0), stacked)
    grad_key, grad_value = [], []
    grad_query = []
    for shared in range(kv_here):
        key_block = kv_own[:, shared * HEAD_SIZE : (shared + 1) * HEAD_SIZE]
        value_at = (kv_here + shared) * HEAD_SIZE
        value_block = kv_own[:, value_at : value_at + HEAD_SIZE]
        heads = [
            slice(head * HEAD_SIZE, (head + 1) * HEAD_SIZE)
            for head in range(shared * per_shared, (shared + 1) * per_shared)
        ]
        queries = jnp.concatenate([query_slots[:, head] for head in heads], axis=0)
        grads = jnp.concatenate([grad_out[:, head] for head in heads], axis=0)
        probs_parts, score_parts = [], []
        for at in range(0, stacked, width):
            scores = matmul(key_block, queries[at : at + width], ROWS_ROWS)
            scores = scores + bias[:, at : at + width]
            highest = jnp.max(scores, axis=0, keepdims=True)
            lifted = jnp.exp2((scores - highest) * exp_scale)
            probs = lifted * (1.0 / jnp.sum(lifted, axis=0, keepdims=True))
            probs_low = probs.astype(BF16)
            grad_probs = matmul(value_block, grads[at : at + width], ROWS_ROWS)
            row_dot = jnp.sum(probs_low.astype(F32) * grad_probs, axis=0, keepdims=True)
            probs_parts.append(probs_low)
            score_parts.append((probs * ((grad_probs - row_dot) * score_scale)).astype(BF16))
        grad_scores = jnp.concatenate(score_parts, axis=1)
        head_query = matmul(grad_scores, key_block, COLS_COLS).astype(BF16)
        for member in range(per_shared):
            grad_query.append(head_query[member * cap : (member + 1) * cap])
        grad_key.append(matmul(grad_scores, queries))
        grad_value.append(matmul(jnp.concatenate(probs_parts, axis=1), grads))
    slot_down = lax.broadcasted_iota(jnp.int32, (slot_count, group_rows), 0).astype(F32)
    slot_to_row = jnp.where(slot_down == recv_row, 1.0, 0.0).astype(BF16)
    grad_slots[pl.ds(pl.multiple_of(owner * cap, 16), cap), :] = jnp.concatenate(grad_query, axis=1)
    grad_own = jnp.concatenate(grad_key + grad_value, axis=1).astype(BF16)
    grad_kv_ref[...] = (
        matmul(slot_to_row, grad_own).astype(BF16).reshape(grad_kv_ref.shape)
    )

    @pl.when(owner == owners - 1)
    def _():
        row = lax.broadcasted_iota(jnp.int32, (group_rows, slot_count), 0).astype(F32)
        place = jnp.where(row == send_row_ref[0:1, :], 1.0, 0.0).astype(BF16)
        grad_query_ref[...] = matmul(place, grad_slots[...]).astype(BF16)


def attention(cap, per_shared, kv_here, row_info, send_cols, send_row, query, upstream, kv_slots):
    owners = row_info.shape[0]
    group_rows, columns = query.shape
    slot_count = owners * cap
    kv_columns = kv_slots.shape[-1]
    whole = lambda array: pl.BlockSpec(array.shape, lambda i: (0,) * array.ndim)
    kv_spec = pl.BlockSpec((owners, None, cap, kv_columns), lambda i: (0, i, 0, 0))
    return pl.pallas_call(
        functools.partial(attention_kernel, cap, per_shared, kv_here),
        grid=(owners,),
        in_specs=[
            pl.BlockSpec((1,) + row_info.shape[1:], lambda i: (i, 0, 0)),
            pl.BlockSpec((1,) + send_cols.shape[1:], lambda i: (i, 0, 0)),
            whole(send_row),
            whole(query),
            whole(upstream),
            kv_spec,
        ],
        out_specs=[whole(query), kv_spec],
        out_shape=[
            jax.ShapeDtypeStruct(query.shape, BF16),
            jax.ShapeDtypeStruct(kv_slots.shape, BF16),
        ],
        scratch_shapes=[pltpu.VMEM((slot_count, columns), BF16)],
        compiler_params=pltpu.CompilerParams(vmem_limit_bytes=VMEM_BYTES),
        name="attention_grads",
    )(row_info, send_cols, send_row, query, upstream, kv_slots)


def mesh_place():
    return lax.axis_index("seq"), lax.axis_index("head")


def ring_place(index, size):
    half = size // 2
    up, side = index // 2, index % 2
    return up + side * (2 * half - 1 - 2 * up)


def ring_index(place, size):
    half = size // 2
    side = place // half
    up = place + side * (2 * half - 1 - 2 * place)
    return up * 2 + side


def remote(src, dst, send_sem, recv_sem, seq, head):
    return pltpu.make_async_remote_copy(
        src_ref=src,
        dst_ref=dst,
        send_sem=send_sem,
        recv_sem=recv_sem,
        device_id=(seq, head),
        device_id_type=pl.DeviceIdType.MESH,
    )


def greet(seq, head, seq_peers, heads):
    barrier = pltpu.get_barrier_semaphore()
    for peer in seq_peers:
        pl.semaphore_signal(
            barrier, inc=1, device_id=(peer, head), device_id_type=pl.DeviceIdType.MESH
        )
    for away in range(1, heads):
        pl.semaphore_signal(
            barrier,
            inc=1,
            device_id=(seq, lax.rem(head + away, heads)),
            device_id_type=pl.DeviceIdType.MESH,
        )
    pl.semaphore_wait(barrier, len(seq_peers) + heads - 1)


def gather_kernel(
    owners,
    heads,
    query_in,
    upstream_in,
    key_in,
    value_in,
    facts_in,
    query_out,
    upstream_out,
    slots_out,
    facts_out,
    kv_out,
    local_sem,
    head_send,
    head_recv,
    facts_send,
    facts_recv,
    ring_send,
    ring_recv,
):
    seq, head = mesh_place()
    tok = query_in.shape[0]
    wide = query_out.shape[1]
    narrow = kv_out.shape[2] // 2
    group_rows = kv_out.shape[1]
    greet(seq, head, [lax.rem(seq + away, owners) for away in range(1, owners)], heads)

    rows = pl.ds(pl.multiple_of(head * tok, tok), tok)

    def columns(peer, width):
        return pl.ds(pl.multiple_of(peer * width, width), width)

    items = [
        (key_in, kv_out.at[seq, rows, pl.ds(0, narrow)], narrow),
        (value_in, kv_out.at[seq, rows, pl.ds(narrow, narrow)], narrow),
        (query_in, query_out.at[rows], wide),
        (upstream_in, upstream_out.at[rows], wide),
    ]
    locals_, sends = [], []
    fact_sends = []

    def send_facts():
        fact_copy = pltpu.make_async_copy(facts_in, facts_out.at[seq], local_sem.at[len(items)])
        fact_copy.start()
        for away in range(1, owners):
            copy = remote(
                facts_in,
                facts_out.at[seq],
                facts_send.at[away - 1],
                facts_recv.at[away - 1],
                lax.rem(seq + away, owners),
                head,
            )
            copy.start()
            fact_sends.append(copy)
        return fact_copy

    for item, (src, dst, width) in enumerate(items):
        if item == 2:
            fact_copy = send_facts()
        copy = pltpu.make_async_copy(src.at[:, columns(head, width)], dst, local_sem.at[item])
        copy.start()
        locals_.append(copy)
        for away in range(1, heads):
            peer = lax.rem(head + away, heads)
            copy = remote(
                src.at[:, columns(peer, width)],
                dst,
                head_send.at[item, away - 1],
                head_recv.at[item, away - 1],
                seq,
                peer,
            )
            copy.start()
            sends.append((item, copy))
    locals_[0].wait()
    locals_[1].wait()
    for item, copy in sends:
        if item < 2:
            copy.wait_recv()

    place = ring_place(seq, owners)
    right = ring_index(lax.rem(place + 1, owners), owners)
    left = ring_index(lax.rem(place + owners - 1, owners), owners)
    part = group_rows // 2
    full = (owners - 1) // 2
    slot_count = slots_out.shape[1]
    every = [(way, chunk) for chunk in range(2) for way in range(2)]
    half_way = [(0, 0), (1, 1)] if owners % 2 == 0 else []

    def shard_at(way, step):
        return ring_index(lax.rem(place + (owners - step if way == 0 else step), owners), owners)

    def hop(way, step, chunk):
        block = kv_out.at[shard_at(way, step), pl.ds(chunk * part, part)]
        return remote(
            block,
            block,
            ring_send.at[way, step, chunk],
            ring_recv.at[way, step, chunk],
            right if way == 0 else left,
            head,
        )

    def pack(shard):
        row = lax.broadcasted_iota(jnp.int32, (group_rows, slot_count), 0).astype(F32)
        send_row = facts_out[shard, 0:1, 0:slot_count]
        spread = jnp.where(row == send_row, 1.0, 0.0).astype(BF16)
        slots_out[shard] = matmul(spread, kv_out[shard], COLS_COLS).astype(BF16)

    for way, chunk in every:
        hop(way, 0, chunk).start()
    fact_copy.wait()
    for copy in fact_sends:
        copy.wait_recv()
    pack(seq)

    def one_step(step, carry):
        for way, chunk in every:
            hop(way, step - 1, chunk).wait_recv()
            hop(way, step, chunk).start()
        for way in range(2):
            pack(shard_at(way, step))
        return carry

    lax.fori_loop(1, full, one_step, 0)
    for way, chunk in every:
        hop(way, full - 1, chunk).wait_recv()
        if (way, chunk) in half_way:
            hop(way, full, chunk).start()
    for way in range(2):
        pack(shard_at(way, full))
    for way, chunk in half_way:
        hop(way, full, chunk).wait_recv()
    if half_way:
        pack(shard_at(0, full + 1))

    def drain(step, carry):
        for way, chunk in every:
            hop(way, step, chunk).wait_send()
        return carry

    lax.fori_loop(0, full, drain, 0)
    for way, chunk in half_way:
        hop(way, full, chunk).wait_send()
    locals_[2].wait()
    locals_[3].wait()
    for item, copy in sends:
        if item >= 2:
            copy.wait_recv()
    for copy in [c for _, c in sends] + fact_sends:
        copy.wait_send()


def gather(owners, heads, slot_count, queries, upstream, keys, values, facts):
    tok = queries.shape[0]
    group_rows = tok * heads
    group = jax.ShapeDtypeStruct((group_rows, queries.shape[1] // heads), BF16)
    kv_columns = 2 * keys.shape[1] // heads
    slots = jax.ShapeDtypeStruct((owners, slot_count, kv_columns), BF16)
    dma = pltpu.SemaphoreType.DMA
    anywhere = pl.BlockSpec(memory_space=pl.ANY)
    vmem = pl.BlockSpec(memory_space=pltpu.VMEM)
    return pl.pallas_call(
        functools.partial(gather_kernel, owners, heads),
        in_specs=[anywhere] * 5,
        out_specs=[anywhere, anywhere, vmem, vmem],
        out_shape=[group, group, slots, jax.ShapeDtypeStruct((owners,) + facts.shape, F32)],
        scratch_shapes=[
            pltpu.VMEM((owners, group_rows, kv_columns), BF16),
            dma((5,)),
            dma((4, heads - 1)),
            dma((4, heads - 1)),
            dma((owners - 1,)),
            dma((owners - 1,)),
            dma((2, owners // 2, 2)),
            dma((2, owners // 2, 2)),
        ],
        compiler_params=pltpu.CompilerParams(
            collective_id=0, has_side_effects=True, vmem_limit_bytes=VMEM_BYTES
        ),
        name="gather_rows",
    )(queries, upstream, keys, values, facts)


def scatter_kernel(
    owners,
    heads,
    send_ref,
    slots_ref,
    query_in,
    query_out,
    key_out,
    value_out,
    sums,
    final,
    local_sem,
    head_send,
    head_recv,
    ring_send,
    ring_recv,
):
    seq, head = mesh_place()
    tok = query_out.shape[0]
    wide = query_in.shape[1]
    group_rows = query_in.shape[0]
    narrow = slots_ref.shape[2] // 2
    slot_count = slots_ref.shape[1]
    part = group_rows // 2
    place = ring_place(seq, owners)
    right = ring_index(lax.rem(place + 1, owners), owners)
    left = ring_index(lax.rem(place + owners - 1, owners), owners)
    greet(seq, head, [right, left], heads)

    def rows_of(peer):
        return pl.ds(pl.multiple_of(peer * tok, tok), tok)

    def exchange(item, src, dst, width):
        mine = dst.at[:, pl.ds(pl.multiple_of(head * width, width), width)]
        local = pltpu.make_async_copy(src.at[rows_of(head)], mine, local_sem.at[item])
        local.start()
        sends = []
        for away in range(1, heads):
            peer = lax.rem(head + away, heads)
            copy = remote(
                src.at[rows_of(peer)],
                mine,
                head_send.at[item, away - 1],
                head_recv.at[item, away - 1],
                seq,
                peer,
            )
            copy.start()
            sends.append(copy)
        return local, sends

    moved = [exchange(0, query_in, query_out, wide)]

    def shard_of(way, step):
        if way == 0:
            return ring_index(lax.rem(place + 2 * owners - 1 - step, owners), owners)
        return ring_index(lax.rem(place + 1 + step, owners), owners)

    def partial_sum(way, step, chunk):
        shard = shard_of(way, step)
        row = lax.broadcasted_iota(jnp.int32, (part, slot_count), 0).astype(F32) + float(chunk * part)
        spread = jnp.where(row == send_ref[shard], 1.0, 0.0).astype(BF16)
        return matmul(spread, slots_ref[shard, :, way * narrow : (way + 1) * narrow])

    def hop(way, step, chunk):
        return remote(
            sums.at[way, step, chunk],
            sums.at[way, step + 1, chunk],
            ring_send.at[way, step, chunk],
            ring_recv.at[way, step, chunk],
            right if way == 0 else left,
            head,
        )

    every = [(way, chunk) for chunk in range(2) for way in range(2)]
    for way, chunk in every:
        sums[way, 0, chunk] = partial_sum(way, 0, chunk).astype(BF16)
        hop(way, 0, chunk).start()

    def one_step(step, carry):
        for way, chunk in every:
            own = partial_sum(way, step, chunk)
            hop(way, step - 1, chunk).wait_recv()
            sums[way, step, chunk] = (own + sums[way, step, chunk].astype(F32)).astype(BF16)
            hop(way, step, chunk).start()
        return carry

    lax.fori_loop(1, owners - 1, one_step, 0)
    for way in range(2):
        for chunk in range(2):
            own = partial_sum(way, owners - 1, chunk)
            hop(way, owners - 2, chunk).wait_recv()
            total = own + sums[way, owners - 1, chunk].astype(F32)
            final[way, chunk * part : (chunk + 1) * part] = total.astype(BF16)
        moved.append(exchange(1 + way, final.at[way], key_out if way == 0 else value_out, narrow))

    def drain(step, carry):
        for way, chunk in every:
            hop(way, step, chunk).wait_send()
        return carry

    lax.fori_loop(0, owners - 1, drain, 0)
    for local, sends in moved:
        local.wait()
        for copy in sends:
            copy.wait()


def scatter(owners, heads, send_all, grad_slots, grad_query):
    group_rows, wide = grad_query.shape
    narrow = grad_slots.shape[2] // 2
    tok = group_rows // heads
    dma = pltpu.SemaphoreType.DMA
    anywhere = pl.BlockSpec(memory_space=pl.ANY)
    vmem = pl.BlockSpec(memory_space=pltpu.VMEM)
    return pl.pallas_call(
        functools.partial(scatter_kernel, owners, heads),
        in_specs=[vmem, vmem, anywhere],
        out_specs=[anywhere] * 3,
        out_shape=[
            jax.ShapeDtypeStruct((tok, wide * heads), BF16),
            jax.ShapeDtypeStruct((tok, narrow * heads), BF16),
            jax.ShapeDtypeStruct((tok, narrow * heads), BF16),
        ],
        scratch_shapes=[
            pltpu.VMEM((2, owners, 2, group_rows // 2, narrow), BF16),
            pltpu.VMEM((2, group_rows, narrow), BF16),
            dma((3,)),
            dma((3, heads - 1)),
            dma((3, heads - 1)),
            dma((2, owners - 1, 2)),
            dma((2, owners - 1, 2)),
        ],
        compiler_params=pltpu.CompilerParams(
            collective_id=1, has_side_effects=True, vmem_limit_bytes=VMEM_BYTES
        ),
        name="scatter_grads",
    )(send_all, grad_slots, grad_query)


def pair_coefficients(doc_gap, pair_docs):
    docs = jnp.arange(doc_gap.shape[0], dtype=jnp.int32)
    chosen = pair_docs[0::2][:, None] == docs[None, :]
    rejected = pair_docs[1::2][:, None] == docs[None, :]
    sign = chosen.astype(F32) - rejected.astype(F32)
    margin = DPO_BETA * jnp.sum(sign * doc_gap[None, :], axis=1)
    weight = DPO_BETA * jax.nn.sigmoid(-margin)
    return -jnp.sum(sign * weight[:, None], axis=0)


def body(
    queries,
    keys,
    values,
    upstream,
    send_rows,
    recv_rows,
    doc_lengths,
    pair_docs,
    response_mask,
    policy_logp,
    ref_logp,
):
    tok_rows = queries.shape[0]
    head_devices = lax.axis_size("head")
    owners = lax.axis_size("seq")
    group_rows = tok_rows * head_devices
    slot_count = send_rows.shape[1]
    cap = slot_count // owners
    kv_heads = keys.shape[1] // HEAD_SIZE
    kv_here = kv_heads // head_devices
    per_shared = queries.shape[1] // keys.shape[1]

    doc_len = doc_lengths[0]
    doc_count = doc_len.shape[0]
    doc_ends = jnp.cumsum(doc_len)
    position = jnp.arange(group_rows, dtype=jnp.int32)
    doc_of_row = jnp.sum((position[:, None] >= doc_ends[None, :]).astype(jnp.int32), axis=1)
    member = doc_of_row[:, None] == jnp.arange(doc_count, dtype=jnp.int32)[None, :]
    token_gap = response_mask.astype(F32) * (policy_logp - ref_logp)
    doc_gap = jnp.sum(jnp.where(member, token_gap[:, None], 0.0), axis=0)
    facts = jnp.concatenate(
        [send_rows[0].astype(F32), recv_rows[0].astype(F32), doc_len.astype(F32), doc_gap]
    )
    facts = jnp.pad(facts, (0, -facts.shape[0] % 128))
    facts = jnp.broadcast_to(facts[None, :], (8, facts.shape[0]))
    query_group, upstream_group, kv_slots, facts = gather(
        owners, head_devices, slot_count, queries, upstream, keys, values, facts
    )
    facts = facts[:, 0]

    send_all = facts[:, :slot_count]
    recv_all = facts[:, slot_count : slot_count + group_rows]
    at = slot_count + group_rows
    len_all = facts[:, at : at + doc_count]
    gap_all = facts[:, at + doc_count : at + 2 * doc_count]
    doc_coef = pair_coefficients(gap_all.reshape(-1), pair_docs).reshape(owners, doc_count)
    ends = jnp.cumsum(len_all, axis=1)
    starts = ends - len_all
    place = jnp.arange(group_rows, dtype=jnp.int32).astype(F32)
    inside = (place[None, :, None] >= starts[:, None, :]) & (place[None, :, None] < ends[:, None, :])
    start_of_row = jnp.sum(jnp.where(inside, starts[:, None, :], 0.0), axis=2)
    coef_of_row = jnp.sum(jnp.where(inside, doc_coef[:, None, :], 0.0), axis=2)
    first_slot = (lax.axis_index("seq") * cap).astype(F32)
    zero = jnp.zeros_like(recv_all)
    row_info = jnp.stack(
        [recv_all, recv_all - first_slot, start_of_row, coef_of_row, zero, zero, zero, zero], axis=1
    )
    own_send = send_rows[0].astype(F32)
    send_cols = jnp.pad(
        own_send.reshape(owners, 1, cap), ((0, 0), (0, 7), (0, -cap % 128)), constant_values=-1.0
    )
    send_row = jnp.broadcast_to(own_send[None, :], (8, slot_count))

    kv_slots = kv_slots.reshape(owners, owners, cap, -1)
    grad_query, grad_slots = attention(
        cap,
        per_shared,
        kv_here,
        row_info,
        send_cols,
        send_row,
        query_group,
        upstream_group,
        kv_slots,
    )

    grad_slots = grad_slots.reshape(owners, slot_count, -1)
    return tuple(
        scatter(owners, head_devices, send_all[:, None, :], grad_slots, grad_query)
    )


def solution(mesh):
    rows = P(("seq", "head"), None)
    return jax.shard_map(
        body,
        mesh=mesh,
        in_specs=(
            rows,
            rows,
            rows,
            rows,
            P("seq", None),
            P("seq", None),
            P("seq", None),
            P(),
            P("seq"),
            P("seq"),
            P("seq"),
        ),
        out_specs=(rows, rows, rows),
        check_vma=False,
    )
```

```python
import functools
import math

import jax
import jax.numpy as jnp
from jax import lax
from jax.experimental import pallas as pl
from jax.experimental.pallas import tpu as pltpu
from jax.sharding import PartitionSpec as P

HEAD_SIZE = 128
DPO_BETA = 0.1
F32 = jnp.float32
BF16 = jnp.bfloat16
VMEM_BYTES = 60 * 1024 * 1024

ROWS_ROWS = (((1,), (1,)), ((), ()))
COLS_COLS = (((0,), (0,)), ((), ()))


def matmul(left, right, dims=(((1,), (0,)), ((), ()))):
    return lax.dot_general(left, right, dims, preferred_element_type=F32)


def mesh_place():
    return lax.axis_index("seq"), lax.axis_index("head")


def ring_place(index, size):
    half = size // 2
    up, side = index // 2, index % 2
    return up + side * (2 * half - 1 - 2 * up)


def ring_index(place, size):
    half = size // 2
    side = place // half
    up = place + side * (2 * half - 1 - 2 * place)
    return up * 2 + side


def remote(src, dst, send_sem, recv_sem, seq, head):
    return pltpu.make_async_remote_copy(
        src_ref=src,
        dst_ref=dst,
        send_sem=send_sem,
        recv_sem=recv_sem,
        device_id=(seq, head),
        device_id_type=pl.DeviceIdType.MESH,
    )


def greet(seq, head, seq_peers, heads):
    barrier = pltpu.get_barrier_semaphore()
    for peer in seq_peers:
        pl.semaphore_signal(
            barrier, inc=1, device_id=(peer, head), device_id_type=pl.DeviceIdType.MESH
        )
    for away in range(1, heads):
        pl.semaphore_signal(
            barrier,
            inc=1,
            device_id=(seq, lax.rem(head + away, heads)),
            device_id_type=pl.DeviceIdType.MESH,
        )
    pl.semaphore_wait(barrier, len(seq_peers) + heads - 1)


def gather_kernel(
    owners,
    heads,
    query_in,
    upstream_in,
    key_in,
    value_in,
    facts_in,
    query_slots,
    upstream_slots,
    slots_out,
    facts_out,
    kv_out,
    query_out,
    upstream_out,
    stage,
    local_sem,
    head_send,
    head_recv,
    facts_send,
    facts_recv,
    ring_send,
    ring_recv,
):
    seq, head = mesh_place()
    tok = query_in.shape[0]
    wide = query_out.shape[1]
    narrow = kv_out.shape[2] // 2
    group_rows = kv_out.shape[1]
    greet(seq, head, [lax.rem(seq + away, owners) for away in range(1, owners)], heads)

    rows = pl.ds(pl.multiple_of(head * tok, tok), tok)

    def columns(peer, width):
        return pl.ds(pl.multiple_of(peer * width, width), width)

    items = [
        (key_in, kv_out.at[seq, rows, pl.ds(0, narrow)], narrow),
        (value_in, kv_out.at[seq, rows, pl.ds(narrow, narrow)], narrow),
        (query_in, query_out.at[rows], wide),
        (upstream_in, upstream_out.at[rows], wide),
    ]
    locals_, sends = [], []
    fact_sends = []

    def send_facts():
        fact_copy = pltpu.make_async_copy(facts_in, facts_out.at[seq], local_sem.at[len(items)])
        fact_copy.start()
        for away in range(1, owners):
            copy = remote(
                facts_in,
                facts_out.at[seq],
                facts_send.at[away - 1],
                facts_recv.at[away - 1],
                lax.rem(seq + away, owners),
                head,
            )
            copy.start()
            fact_sends.append(copy)
        return fact_copy

    for item, (src, dst, width) in enumerate(items):
        if item == 2:
            fact_copy = send_facts()
        copy = pltpu.make_async_copy(src.at[:, columns(head, width)], dst, local_sem.at[item])
        copy.start()
        locals_.append(copy)
        for away in range(1, heads):
            peer = lax.rem(head + away, heads)
            copy = remote(
                src.at[:, columns(peer, width)],
                dst,
                head_send.at[item, away - 1],
                head_recv.at[item, away - 1],
                seq,
                peer,
            )
            copy.start()
            sends.append((item, copy))
    locals_[0].wait()
    locals_[1].wait()
    for item, copy in sends:
        if item < 2:
            copy.wait_recv()

    place = ring_place(seq, owners)
    right = ring_index(lax.rem(place + 1, owners), owners)
    left = ring_index(lax.rem(place + owners - 1, owners), owners)
    part = group_rows // 2
    full = (owners - 1) // 2
    slot_count = slots_out.shape[1]
    every = [(way, chunk) for chunk in range(2) for way in range(2)]
    half_way = [(0, 0), (1, 1)] if owners % 2 == 0 else []

    def shard_at(way, step):
        return ring_index(lax.rem(place + (owners - step if way == 0 else step), owners), owners)

    def hop(way, step, chunk):
        block = kv_out.at[shard_at(way, step), pl.ds(chunk * part, part)]
        return remote(
            block,
            block,
            ring_send.at[way, step, chunk],
            ring_recv.at[way, step, chunk],
            right if way == 0 else left,
            head,
        )

    def spread_of(shard):
        row = lax.broadcasted_iota(jnp.int32, (group_rows, slot_count), 0).astype(F32)
        send_row = facts_out[shard, 0:1, 0:slot_count]
        return jnp.where(row == send_row, 1.0, 0.0).astype(BF16)

    def pack(shard):
        stage[...] = matmul(spread_of(shard), kv_out[shard], COLS_COLS).astype(BF16)
        copy = pltpu.make_async_copy(stage, slots_out.at[shard], local_sem.at[len(items) + 1])
        copy.start()
        copy.wait()

    for way, chunk in every:
        hop(way, 0, chunk).start()
    fact_copy.wait()
    for copy in fact_sends:
        copy.wait_recv()
    pack(seq)

    def one_step(step, carry):
        for way, chunk in every:
            hop(way, step - 1, chunk).wait_recv()
            hop(way, step, chunk).start()
        for way in range(2):
            pack(shard_at(way, step))
        return carry

    lax.fori_loop(1, full, one_step, 0)
    for way, chunk in every:
        hop(way, full - 1, chunk).wait_recv()
        if (way, chunk) in half_way:
            hop(way, full, chunk).start()
    for way in range(2):
        pack(shard_at(way, full))
    locals_[2].wait()
    locals_[3].wait()
    for item, copy in sends:
        if item >= 2:
            copy.wait_recv()
    spread = spread_of(seq)
    query_slots[...] = matmul(spread, query_out[...], COLS_COLS).astype(BF16)
    upstream_slots[...] = matmul(spread, upstream_out[...], COLS_COLS).astype(BF16)
    for way, chunk in half_way:
        hop(way, full, chunk).wait_recv()
    if half_way:
        pack(shard_at(0, full + 1))

    def drain(step, carry):
        for way, chunk in every:
            hop(way, step, chunk).wait_send()
        return carry

    lax.fori_loop(0, full, drain, 0)
    for way, chunk in half_way:
        hop(way, full, chunk).wait_send()
    for copy in [c for _, c in sends] + fact_sends:
        copy.wait_send()


def gather(owners, heads, slot_count, queries, upstream, keys, values, facts):
    tok = queries.shape[0]
    group_rows = tok * heads
    wide = queries.shape[1] // heads
    group = jax.ShapeDtypeStruct((slot_count, wide), BF16)
    kv_columns = 2 * keys.shape[1] // heads
    slots = jax.ShapeDtypeStruct((owners, slot_count, kv_columns), BF16)
    dma = pltpu.SemaphoreType.DMA
    anywhere = pl.BlockSpec(memory_space=pl.ANY)
    vmem = pl.BlockSpec(memory_space=pltpu.VMEM)
    return pl.pallas_call(
        functools.partial(gather_kernel, owners, heads),
        in_specs=[anywhere] * 5,
        out_specs=[vmem, vmem, anywhere, vmem],
        out_shape=[group, group, slots, jax.ShapeDtypeStruct((owners,) + facts.shape, F32)],
        scratch_shapes=[
            pltpu.VMEM((owners, group_rows, kv_columns), BF16),
            pltpu.VMEM((group_rows, wide), BF16),
            pltpu.VMEM((group_rows, wide), BF16),
            pltpu.VMEM((slot_count, kv_columns), BF16),
            dma((6,)),
            dma((4, heads - 1)),
            dma((4, heads - 1)),
            dma((owners - 1,)),
            dma((owners - 1,)),
            dma((2, owners // 2, 2)),
            dma((2, owners // 2, 2)),
        ],
        compiler_params=pltpu.CompilerParams(
            collective_id=0, has_side_effects=True, vmem_limit_bytes=VMEM_BYTES
        ),
        name="gather_rows",
    )(queries, upstream, keys, values, facts)


def grads_kernel(
    owners,
    heads,
    cap,
    per_shared,
    row_info_ref,
    send_row_ref,
    query_ref,
    upstream_ref,
    key_ref,
    value_ref,
    send_ref,
    query_out,
    key_out,
    value_out,
    query_slots,
    query_rows,
    grad_slots,
    sums,
    final,
    local_sem,
    head_send,
    head_recv,
    ring_send,
    ring_recv,
):
    shared, owner = pl.program_id(0), pl.program_id(1)
    kv_here = key_out.shape[1] // heads // HEAD_SIZE
    seq, head = mesh_place()
    tok = query_out.shape[0]
    group_rows = tok * heads
    slot_count = owners * cap
    wide = per_shared * HEAD_SIZE
    part = group_rows // 2
    place = ring_place(seq, owners)
    right = ring_index(lax.rem(place + 1, owners), owners)
    left = ring_index(lax.rem(place + owners - 1, owners), owners)

    @pl.when((shared == 0) & (owner == 0))
    def _():
        greet(seq, head, [right, left], heads)

    def rows_of(peer):
        return pl.ds(pl.multiple_of(peer * tok, tok), tok)

    def exchange(item, which):
        src = query_rows.at[which] if item == 0 else final.at[which, item - 1]
        dst = (query_out, key_out, value_out)[item]
        width = wide if item == 0 else HEAD_SIZE
        at = pl.multiple_of((head * kv_here + which) * width, width)
        mine = dst.at[:, pl.ds(at, width)]
        local = pltpu.make_async_copy(src.at[rows_of(head)], mine, local_sem.at[which, item])
        sends = []
        for away in range(1, heads):
            peer = lax.rem(head + away, heads)
            sends.append(
                remote(
                    src.at[rows_of(peer)],
                    mine,
                    head_send.at[which, item, away - 1],
                    head_recv.at[which, item, away - 1],
                    seq,
                    peer,
                )
            )
        return [local] + sends

    def shard_of(way, step):
        if way == 0:
            return ring_index(lax.rem(place + 2 * owners - 1 - step, owners), owners)
        return ring_index(lax.rem(place + 1 + step, owners), owners)

    def partial_sum(which, way, step, chunk):
        shard = shard_of(way, step)
        row = lax.broadcasted_iota(jnp.int32, (part, slot_count), 0).astype(F32) + float(chunk * part)
        spread = jnp.where(row == send_ref[shard], 1.0, 0.0).astype(BF16)
        return matmul(
            spread, grad_slots[which, shard, :, way * HEAD_SIZE : (way + 1) * HEAD_SIZE]
        )

    def hop(which, way, step, chunk):
        return remote(
            sums.at[which, way, step, chunk],
            sums.at[which, way, step + 1, chunk],
            ring_send.at[which, way, step, chunk],
            ring_recv.at[which, way, step, chunk],
            right if way == 0 else left,
            head,
        )

    every = [(way, chunk) for chunk in range(2) for way in range(2)]

    def ring_first(which):
        for way, chunk in every:
            sums[which, way, 0, chunk] = partial_sum(which, way, 0, chunk).astype(BF16)
            hop(which, way, 0, chunk).start()

    def ring_middle(which, step):
        for way, chunk in every:
            own = partial_sum(which, way, step, chunk)
            hop(which, way, step - 1, chunk).wait_recv()
            total = own + sums[which, way, step, chunk].astype(F32)
            sums[which, way, step, chunk] = total.astype(BF16)
            hop(which, way, step, chunk).start()

    def ring_last(which):
        for way in range(2):
            for chunk in range(2):
                own = partial_sum(which, way, owners - 1, chunk)
                hop(which, way, owners - 2, chunk).wait_recv()
                total = own + sums[which, way, owners - 1, chunk].astype(F32)
                final[which, way, chunk * part : (chunk + 1) * part] = total.astype(BF16)
            for copy in exchange(1 + way, which):
                copy.start()

    @pl.when((shared > 0) & (owner == 0))
    def _():
        ring_first(shared - 1)

    @pl.when((shared > 0) & (owner > 0) & (owner < owners - 1))
    def _():
        ring_middle(shared - 1, owner)

    @pl.when((shared > 0) & (owner == owners - 1))
    def _():
        ring_last(shared - 1)

    info = row_info_ref[0]
    recv_row = info[0:1, :]
    local_row = info[1:2, :]
    coef_row = info[3:4, :]
    columns_of = jnp.transpose(info)
    recv_column = columns_of[:, 0:1]
    local_column = columns_of[:, 1:2]
    start_column = columns_of[:, 2:3]

    slot_lane = lax.broadcasted_iota(jnp.int32, (group_rows, slot_count), 1).astype(F32)
    row_to_slot = jnp.where(slot_lane == recv_column, 1.0, 0.0).astype(BF16)
    kv_slots = jnp.concatenate([key_ref[...], value_ref[...]], axis=-1)
    kv_own = matmul(row_to_slot, kv_slots.reshape(slot_count, 2 * HEAD_SIZE)).astype(BF16)
    key_block = kv_own[:, :HEAD_SIZE]
    value_block = kv_own[:, HEAD_SIZE:]

    lane = lax.broadcasted_iota(jnp.int32, (cap, group_rows), 0).astype(F32)
    coef = jnp.sum(jnp.where(lane == local_row, coef_row, 0.0), axis=1, keepdims=True)
    grad_out = (coef * upstream_ref[...].astype(F32)).astype(BF16)

    across = lax.broadcasted_iota(jnp.int32, (group_rows, cap), 1).astype(F32)
    down = lax.broadcasted_iota(jnp.int32, (group_rows, cap), 0).astype(F32)
    mine = across == local_column
    position = jnp.sum(jnp.where(mine, down, 0.0), axis=0, keepdims=True)
    start = jnp.sum(jnp.where(mine, start_column, 0.0), axis=0, keepdims=True)
    stacked = per_shared * cap
    position = jnp.concatenate([position] * per_shared, axis=1)
    start = jnp.concatenate([start] * per_shared, axis=1)

    score_scale = 1.0 / math.sqrt(HEAD_SIZE)
    exp_scale = score_scale * math.log2(math.e)
    width = next((w for w in (256, 128) if stacked % w == 0), stacked)
    key_row = lax.broadcasted_iota(jnp.int32, (group_rows, width), 0).astype(F32)
    columns = [slice(i * HEAD_SIZE, (i + 1) * HEAD_SIZE) for i in range(per_shared)]
    queries = jnp.concatenate([query_ref[:, c] for c in columns], axis=0)
    grads = jnp.concatenate([grad_out[:, c] for c in columns], axis=0)
    probs_parts, score_parts = [], []
    for at in range(0, stacked, width):
        scores = matmul(key_block, queries[at : at + width], ROWS_ROWS)
        allowed = (key_row >= start[:, at : at + width]) & (key_row <= position[:, at : at + width])
        scores = jnp.where(allowed, scores, -1e30)
        highest = jnp.max(scores, axis=0, keepdims=True)
        lifted = jnp.exp2((scores - highest) * exp_scale)
        probs = lifted * (1.0 / jnp.sum(lifted, axis=0, keepdims=True))
        probs_low = probs.astype(BF16)
        grad_probs = matmul(value_block, grads[at : at + width], ROWS_ROWS)
        row_dot = jnp.sum(probs_low.astype(F32) * grad_probs, axis=0, keepdims=True)
        probs_parts.append(probs_low)
        score_parts.append((probs * ((grad_probs - row_dot) * score_scale)).astype(BF16))
    grad_scores = jnp.concatenate(score_parts, axis=1)
    head_query = matmul(grad_scores, key_block, COLS_COLS).astype(BF16)
    query_slots[pl.ds(pl.multiple_of(owner * cap, 16), cap), :] = jnp.concatenate(
        [head_query[i * cap : (i + 1) * cap] for i in range(per_shared)], axis=1
    )
    grad_key = matmul(grad_scores, queries)
    grad_value = matmul(jnp.concatenate(probs_parts, axis=1), grads)
    grad_own = jnp.concatenate([grad_key, grad_value], axis=1).astype(BF16)
    slot_down = lax.broadcasted_iota(jnp.int32, (slot_count, group_rows), 0).astype(F32)
    slot_to_row = jnp.where(slot_down == recv_row, 1.0, 0.0).astype(BF16)
    grad_back = matmul(slot_to_row, grad_own).astype(BF16)
    for source in range(owners):
        grad_slots[shared, source, pl.ds(pl.multiple_of(owner * cap, 16), cap), :] = grad_back[
            source * cap : (source + 1) * cap
        ]

    @pl.when(owner == owners - 1)
    def _():
        row = lax.broadcasted_iota(jnp.int32, (group_rows, slot_count), 0).astype(F32)
        spread = jnp.where(row == send_row_ref[0:1, :], 1.0, 0.0).astype(BF16)
        query_rows[shared] = matmul(spread, query_slots[...]).astype(BF16)
        for copy in exchange(0, shared):
            copy.start()

    @pl.when((shared == kv_here - 1) & (owner == owners - 1))
    def _():
        ring_first(kv_here - 1)

        def one_step(step, carry):
            ring_middle(kv_here - 1, step)
            return carry

        lax.fori_loop(1, owners - 1, one_step, 0)
        ring_last(kv_here - 1)

        def drain(step, carry):
            for which in range(kv_here):
                for way, chunk in every:
                    hop(which, way, step, chunk).wait_send()
            return carry

        lax.fori_loop(0, owners - 1, drain, 0)
        for which in range(kv_here):
            for item in range(3):
                for copy in exchange(item, which):
                    copy.wait()


def grads(owners, heads, cap, per_shared, row_info, send_row, query, upstream, kv_slots, send_all):
    slot_count = owners * cap
    kv_here = kv_slots.shape[-1] // HEAD_SIZE // 2
    wide = per_shared * HEAD_SIZE
    group_rows = row_info.shape[2]
    tok = group_rows // heads
    dma = pltpu.SemaphoreType.DMA
    anywhere = pl.BlockSpec(memory_space=pl.ANY)
    vmem = pl.BlockSpec(memory_space=pltpu.VMEM)
    rows_spec = pl.BlockSpec((cap, wide), lambda g, i: (i, g))

    def kv_spec(shift):
        return pl.BlockSpec((owners, None, cap, HEAD_SIZE), lambda g, i: (0, i, 0, g + shift))

    return pl.pallas_call(
        functools.partial(grads_kernel, owners, heads, cap, per_shared),
        grid=(kv_here, owners),
        in_specs=[
            pl.BlockSpec((1,) + row_info.shape[1:], lambda g, i: (i, 0, 0)),
            vmem,
            rows_spec,
            rows_spec,
            kv_spec(0),
            kv_spec(kv_here),
            vmem,
        ],
        out_specs=[anywhere] * 3,
        out_shape=[
            jax.ShapeDtypeStruct((tok, kv_here * wide * heads), BF16),
            jax.ShapeDtypeStruct((tok, kv_here * HEAD_SIZE * heads), BF16),
            jax.ShapeDtypeStruct((tok, kv_here * HEAD_SIZE * heads), BF16),
        ],
        scratch_shapes=[
            pltpu.VMEM((slot_count, wide), BF16),
            pltpu.VMEM((kv_here, group_rows, wide), BF16),
            pltpu.VMEM((kv_here, owners, slot_count, 2 * HEAD_SIZE), BF16),
            pltpu.VMEM((kv_here, 2, owners, 2, group_rows // 2, HEAD_SIZE), BF16),
            pltpu.VMEM((kv_here, 2, group_rows, HEAD_SIZE), BF16),
            dma((kv_here, 3)),
            dma((kv_here, 3, heads - 1)),
            dma((kv_here, 3, heads - 1)),
            dma((kv_here, 2, owners - 1, 2)),
            dma((kv_here, 2, owners - 1, 2)),
        ],
        compiler_params=pltpu.CompilerParams(
            collective_id=1, has_side_effects=True, vmem_limit_bytes=VMEM_BYTES
        ),
        name="attention_grads",
    )(row_info, send_row, query, upstream, kv_slots, kv_slots, send_all)


def pair_coefficients(doc_gap, pair_docs):
    docs = jnp.arange(doc_gap.shape[0], dtype=jnp.int32)
    chosen = pair_docs[0::2][:, None] == docs[None, :]
    rejected = pair_docs[1::2][:, None] == docs[None, :]
    sign = chosen.astype(F32) - rejected.astype(F32)
    margin = DPO_BETA * jnp.sum(sign * doc_gap[None, :], axis=1)
    weight = DPO_BETA * jax.nn.sigmoid(-margin)
    return -jnp.sum(sign * weight[:, None], axis=0)


def body(
    queries,
    keys,
    values,
    upstream,
    send_rows,
    recv_rows,
    doc_lengths,
    pair_docs,
    response_mask,
    policy_logp,
    ref_logp,
):
    tok_rows = queries.shape[0]
    head_devices = lax.axis_size("head")
    owners = lax.axis_size("seq")
    group_rows = tok_rows * head_devices
    slot_count = send_rows.shape[1]
    cap = slot_count // owners
    per_shared = queries.shape[1] // keys.shape[1]

    doc_len = doc_lengths[0]
    doc_count = doc_len.shape[0]
    doc_ends = jnp.cumsum(doc_len)
    position = jnp.arange(group_rows, dtype=jnp.int32)
    doc_of_row = jnp.sum((position[:, None] >= doc_ends[None, :]).astype(jnp.int32), axis=1)
    member = doc_of_row[:, None] == jnp.arange(doc_count, dtype=jnp.int32)[None, :]
    token_gap = response_mask.astype(F32) * (policy_logp - ref_logp)
    doc_gap = jnp.sum(jnp.where(member, token_gap[:, None], 0.0), axis=0)
    facts = jnp.concatenate(
        [send_rows[0].astype(F32), recv_rows[0].astype(F32), doc_len.astype(F32), doc_gap]
    )
    facts = jnp.pad(facts, (0, -facts.shape[0] % 128))
    facts = jnp.broadcast_to(facts[None, :], (8, facts.shape[0]))
    query_slots, upstream_slots, kv_slots, facts = gather(
        owners, head_devices, slot_count, queries, upstream, keys, values, facts
    )
    facts = facts[:, 0]

    send_all = facts[:, :slot_count]
    recv_all = facts[:, slot_count : slot_count + group_rows]
    at = slot_count + group_rows
    len_all = facts[:, at : at + doc_count]
    gap_all = facts[:, at + doc_count : at + 2 * doc_count]
    doc_coef = pair_coefficients(gap_all.reshape(-1), pair_docs).reshape(owners, doc_count)
    ends = jnp.cumsum(len_all, axis=1)
    starts = ends - len_all
    place = jnp.arange(group_rows, dtype=jnp.int32).astype(F32)
    inside = (place[None, :, None] >= starts[:, None, :]) & (place[None, :, None] < ends[:, None, :])
    start_of_row = jnp.sum(jnp.where(inside, starts[:, None, :], 0.0), axis=2)
    coef_of_row = jnp.sum(jnp.where(inside, doc_coef[:, None, :], 0.0), axis=2)
    first_slot = (lax.axis_index("seq") * cap).astype(F32)
    zero = jnp.zeros_like(recv_all)
    row_info = jnp.stack(
        [recv_all, recv_all - first_slot, start_of_row, coef_of_row, zero, zero, zero, zero], axis=1
    )
    own_send = send_rows[0].astype(F32)
    send_row = jnp.broadcast_to(own_send[None, :], (8, slot_count))

    kv_slots = kv_slots.reshape(owners, owners, cap, -1)
    return tuple(
        grads(
            owners,
            head_devices,
            cap,
            per_shared,
            row_info,
            send_row,
            query_slots,
            upstream_slots,
            kv_slots,
            send_all[:, None, :],
        )
    )


def solution(mesh):
    rows = P(("seq", "head"), None)
    return jax.shard_map(
        body,
        mesh=mesh,
        in_specs=(
            rows,
            rows,
            rows,
            rows,
            P("seq", None),
            P("seq", None),
            P("seq", None),
            P(),
            P("seq"),
            P("seq"),
            P("seq"),
        ),
        out_specs=(rows, rows, rows),
        check_vma=False,
    )
```

```python
import functools
import math

import jax
import jax.numpy as jnp
from jax import lax
from jax.experimental import pallas as pl
from jax.experimental.pallas import tpu as pltpu
from jax.sharding import PartitionSpec as P

HEAD_SIZE = 128
DPO_BETA = 0.1
F32 = jnp.float32
BF16 = jnp.bfloat16
VMEM_BYTES = 60 * 1024 * 1024

ROWS_ROWS = (((1,), (1,)), ((), ()))
COLS_COLS = (((0,), (0,)), ((), ()))


def matmul(left, right, dims=(((1,), (0,)), ((), ()))):
    return lax.dot_general(left, right, dims, preferred_element_type=F32)


def mesh_place():
    return lax.axis_index("seq"), lax.axis_index("head")


def ring_place(index, size):
    half = size // 2
    up, side = index // 2, index % 2
    return up + side * (2 * half - 1 - 2 * up)


def ring_index(place, size):
    half = size // 2
    side = place // half
    up = place + side * (2 * half - 1 - 2 * place)
    return up * 2 + side


def remote(src, dst, send_sem, recv_sem, seq, head):
    return pltpu.make_async_remote_copy(
        src_ref=src,
        dst_ref=dst,
        send_sem=send_sem,
        recv_sem=recv_sem,
        device_id=(seq, head),
        device_id_type=pl.DeviceIdType.MESH,
    )


def greet(seq, head, seq_peers, heads):
    barrier = pltpu.get_barrier_semaphore()
    for peer in seq_peers:
        pl.semaphore_signal(
            barrier, inc=1, device_id=(peer, head), device_id_type=pl.DeviceIdType.MESH
        )
    for away in range(1, heads):
        pl.semaphore_signal(
            barrier,
            inc=1,
            device_id=(seq, lax.rem(head + away, heads)),
            device_id_type=pl.DeviceIdType.MESH,
        )
    pl.semaphore_wait(barrier, len(seq_peers) + heads - 1)


def gather_kernel(
    owners,
    heads,
    query_in,
    upstream_in,
    key_in,
    value_in,
    facts_in,
    query_slots,
    upstream_slots,
    slots_out,
    facts_out,
    kv_out,
    query_out,
    upstream_out,
    stage,
    local_sem,
    head_send,
    head_recv,
    facts_send,
    facts_recv,
    ring_send,
    ring_recv,
):
    seq, head = mesh_place()
    tok = query_in.shape[0]
    wide = query_out.shape[1]
    narrow = kv_out.shape[2] // 2
    group_rows = kv_out.shape[1]
    greet(seq, head, [lax.rem(seq + away, owners) for away in range(1, owners)], heads)

    rows = pl.ds(pl.multiple_of(head * tok, tok), tok)

    def columns(peer, width):
        return pl.ds(pl.multiple_of(peer * width, width), width)

    items = [
        (key_in, kv_out.at[seq, rows, pl.ds(0, narrow)], narrow),
        (value_in, kv_out.at[seq, rows, pl.ds(narrow, narrow)], narrow),
        (query_in, query_out.at[rows], wide),
        (upstream_in, upstream_out.at[rows], wide),
    ]
    locals_, sends = [], []
    fact_sends = []

    def send_facts():
        fact_copy = pltpu.make_async_copy(facts_in, facts_out.at[seq], local_sem.at[len(items)])
        fact_copy.start()
        for away in range(1, owners):
            copy = remote(
                facts_in,
                facts_out.at[seq],
                facts_send.at[away - 1],
                facts_recv.at[away - 1],
                lax.rem(seq + away, owners),
                head,
            )
            copy.start()
            fact_sends.append(copy)
        return fact_copy

    for item, (src, dst, width) in enumerate(items):
        if item == 2:
            fact_copy = send_facts()
        copy = pltpu.make_async_copy(src.at[:, columns(head, width)], dst, local_sem.at[item])
        copy.start()
        locals_.append(copy)
        for away in range(1, heads):
            peer = lax.rem(head + away, heads)
            copy = remote(
                src.at[:, columns(peer, width)],
                dst,
                head_send.at[item, away - 1],
                head_recv.at[item, away - 1],
                seq,
                peer,
            )
            copy.start()
            sends.append((item, copy))
    locals_[0].wait()
    locals_[1].wait()
    for item, copy in sends:
        if item < 2:
            copy.wait_recv()

    place = ring_place(seq, owners)
    right = ring_index(lax.rem(place + 1, owners), owners)
    left = ring_index(lax.rem(place + owners - 1, owners), owners)
    part = group_rows // 2
    full = (owners - 1) // 2
    slot_count = slots_out.shape[1]
    every = [(way, chunk) for chunk in range(2) for way in range(2)]
    half_way = [(0, 0), (1, 1)] if owners % 2 == 0 else []

    def shard_at(way, step):
        return ring_index(lax.rem(place + (owners - step if way == 0 else step), owners), owners)

    def hop(way, step, chunk):
        block = kv_out.at[shard_at(way, step), pl.ds(chunk * part, part)]
        return remote(
            block,
            block,
            ring_send.at[way, step, chunk],
            ring_recv.at[way, step, chunk],
            right if way == 0 else left,
            head,
        )

    def spread_of(shard):
        row = lax.broadcasted_iota(jnp.int32, (group_rows, slot_count), 0).astype(F32)
        send_row = facts_out[shard, 0:1, 0:slot_count]
        return jnp.where(row == send_row, 1.0, 0.0).astype(BF16)

    def pack(shard):
        stage[...] = matmul(spread_of(shard), kv_out[shard], COLS_COLS).astype(BF16)
        copy = pltpu.make_async_copy(stage, slots_out.at[shard], local_sem.at[len(items) + 1])
        copy.start()
        copy.wait()

    for way, chunk in every:
        hop(way, 0, chunk).start()
    fact_copy.wait()
    for copy in fact_sends:
        copy.wait_recv()
    pack(seq)

    def one_step(step, carry):
        for way, chunk in every:
            hop(way, step - 1, chunk).wait_recv()
            hop(way, step, chunk).start()
        for way in range(2):
            pack(shard_at(way, step))
        return carry

    lax.fori_loop(1, full, one_step, 0)
    for way, chunk in every:
        hop(way, full - 1, chunk).wait_recv()
        if (way, chunk) in half_way:
            hop(way, full, chunk).start()
    for way in range(2):
        pack(shard_at(way, full))
    locals_[2].wait()
    locals_[3].wait()
    for item, copy in sends:
        if item >= 2:
            copy.wait_recv()
    spread = spread_of(seq)
    query_slots[...] = matmul(spread, query_out[...], COLS_COLS).astype(BF16)
    upstream_slots[...] = matmul(spread, upstream_out[...], COLS_COLS).astype(BF16)
    for way, chunk in half_way:
        hop(way, full, chunk).wait_recv()
    if half_way:
        pack(shard_at(0, full + 1))

    def drain(step, carry):
        for way, chunk in every:
            hop(way, step, chunk).wait_send()
        return carry

    lax.fori_loop(0, full, drain, 0)
    for way, chunk in half_way:
        hop(way, full, chunk).wait_send()
    for copy in [c for _, c in sends] + fact_sends:
        copy.wait_send()


def gather(owners, heads, slot_count, queries, upstream, keys, values, facts):
    tok = queries.shape[0]
    group_rows = tok * heads
    wide = queries.shape[1] // heads
    group = jax.ShapeDtypeStruct((slot_count, wide), BF16)
    kv_columns = 2 * keys.shape[1] // heads
    slots = jax.ShapeDtypeStruct((owners, slot_count, kv_columns), BF16)
    dma = pltpu.SemaphoreType.DMA
    anywhere = pl.BlockSpec(memory_space=pl.ANY)
    vmem = pl.BlockSpec(memory_space=pltpu.VMEM)
    return pl.pallas_call(
        functools.partial(gather_kernel, owners, heads),
        in_specs=[anywhere] * 5,
        out_specs=[vmem, vmem, anywhere, vmem],
        out_shape=[group, group, slots, jax.ShapeDtypeStruct((owners,) + facts.shape, F32)],
        scratch_shapes=[
            pltpu.VMEM((owners, group_rows, kv_columns), BF16),
            pltpu.VMEM((group_rows, wide), BF16),
            pltpu.VMEM((group_rows, wide), BF16),
            pltpu.VMEM((slot_count, kv_columns), BF16),
            dma((6,)),
            dma((4, heads - 1)),
            dma((4, heads - 1)),
            dma((owners - 1,)),
            dma((owners - 1,)),
            dma((2, owners // 2, 2)),
            dma((2, owners // 2, 2)),
        ],
        compiler_params=pltpu.CompilerParams(
            collective_id=0, has_side_effects=True, vmem_limit_bytes=VMEM_BYTES
        ),
        name="gather_rows",
    )(queries, upstream, keys, values, facts)


def grads_kernel(
    owners,
    heads,
    cap,
    per_shared,
    row_info_ref,
    send_row_ref,
    query_ref,
    upstream_ref,
    key_ref,
    value_ref,
    send_ref,
    query_out,
    key_out,
    value_out,
    query_slots,
    query_rows,
    grad_slots,
    sums,
    final,
    local_sem,
    head_send,
    head_recv,
    ring_send,
    ring_recv,
):
    shared, owner = pl.program_id(0), pl.program_id(1)
    kv_here = key_out.shape[1] // heads // HEAD_SIZE
    seq, head = mesh_place()
    tok = query_out.shape[0]
    group_rows = tok * heads
    slot_count = owners * cap
    wide = per_shared * HEAD_SIZE
    part = group_rows // 2
    place = ring_place(seq, owners)
    right = ring_index(lax.rem(place + 1, owners), owners)
    left = ring_index(lax.rem(place + owners - 1, owners), owners)

    @pl.when((shared == 0) & (owner == 0))
    def _():
        greet(seq, head, [right, left], heads)

    def rows_of(peer):
        return pl.ds(pl.multiple_of(peer * tok, tok), tok)

    def exchange(item, which):
        src = query_rows.at[which] if item == 0 else final.at[which, item - 1]
        dst = (query_out, key_out, value_out)[item]
        width = wide if item == 0 else HEAD_SIZE
        at = pl.multiple_of((head * kv_here + which) * width, width)
        mine = dst.at[:, pl.ds(at, width)]
        local = pltpu.make_async_copy(src.at[rows_of(head)], mine, local_sem.at[which, item])
        sends = []
        for away in range(1, heads):
            peer = lax.rem(head + away, heads)
            sends.append(
                remote(
                    src.at[rows_of(peer)],
                    mine,
                    head_send.at[which, item, away - 1],
                    head_recv.at[which, item, away - 1],
                    seq,
                    peer,
                )
            )
        return [local] + sends

    def shard_of(way, step):
        if way == 0:
            return ring_index(lax.rem(place + 2 * owners - 1 - step, owners), owners)
        return ring_index(lax.rem(place + 1 + step, owners), owners)

    def put_in_rows(which, shard):
        row = lax.broadcasted_iota(jnp.int32, (group_rows, slot_count), 0).astype(F32)
        spread = jnp.where(row == send_ref[shard], 1.0, 0.0).astype(BF16)
        placed = matmul(spread, grad_slots[which, shard]).astype(BF16)
        grad_slots[which, shard, 0:group_rows, :] = placed

    def partial_sum(which, way, step, chunk):
        return grad_slots[
            which,
            shard_of(way, step),
            chunk * part : (chunk + 1) * part,
            way * HEAD_SIZE : (way + 1) * HEAD_SIZE,
        ]

    def hop(which, way, step, chunk):
        return remote(
            sums.at[which, way, step, chunk],
            sums.at[which, way, step + 1, chunk],
            ring_send.at[which, way, step, chunk],
            ring_recv.at[which, way, step, chunk],
            right if way == 0 else left,
            head,
        )

    every = [(way, chunk) for chunk in range(2) for way in range(2)]

    def ring_first(which):
        put_in_rows(which, shard_of(0, 0))
        if owners > 2:
            put_in_rows(which, shard_of(1, 0))
        for way, chunk in every:
            sums[which, way, 0, chunk] = partial_sum(which, way, 0, chunk)
            hop(which, way, 0, chunk).start()

    def ring_middle(which, step):
        @pl.when(step < owners // 2)
        def _():
            put_in_rows(which, shard_of(0, step))

        @pl.when(step < owners // 2 - 1)
        def _():
            put_in_rows(which, shard_of(1, step))

        for way, chunk in every:
            own = partial_sum(which, way, step, chunk).astype(F32)
            hop(which, way, step - 1, chunk).wait_recv()
            total = own + sums[which, way, step, chunk].astype(F32)
            sums[which, way, step, chunk] = total.astype(BF16)
            hop(which, way, step, chunk).start()

    def ring_last(which):
        put_in_rows(which, seq)
        for way in range(2):
            for chunk in range(2):
                own = partial_sum(which, way, owners - 1, chunk).astype(F32)
                hop(which, way, owners - 2, chunk).wait_recv()
                total = own + sums[which, way, owners - 1, chunk].astype(F32)
                final[which, way, chunk * part : (chunk + 1) * part] = total.astype(BF16)
            for copy in exchange(1 + way, which):
                copy.start()

    @pl.when((shared > 0) & (owner == 0))
    def _():
        ring_first(shared - 1)

    @pl.when((shared > 0) & (owner > 0) & (owner < owners - 1))
    def _():
        ring_middle(shared - 1, owner)

    @pl.when((shared > 0) & (owner == owners - 1))
    def _():
        ring_last(shared - 1)

    info = row_info_ref[0]
    recv_row = info[0:1, :]
    local_row = info[1:2, :]
    coef_row = info[3:4, :]
    columns_of = jnp.transpose(info)
    recv_column = columns_of[:, 0:1]
    local_column = columns_of[:, 1:2]
    start_column = columns_of[:, 2:3]

    slot_lane = lax.broadcasted_iota(jnp.int32, (group_rows, slot_count), 1).astype(F32)
    row_to_slot = jnp.where(slot_lane == recv_column, 1.0, 0.0).astype(BF16)
    kv_slots = jnp.concatenate([key_ref[...], value_ref[...]], axis=-1)
    kv_own = matmul(row_to_slot, kv_slots.reshape(slot_count, 2 * HEAD_SIZE)).astype(BF16)
    key_block = kv_own[:, :HEAD_SIZE]
    value_block = kv_own[:, HEAD_SIZE:]

    lane = lax.broadcasted_iota(jnp.int32, (cap, group_rows), 0).astype(F32)
    coef = jnp.sum(jnp.where(lane == local_row, coef_row, 0.0), axis=1, keepdims=True)
    grad_out = (coef * upstream_ref[...].astype(F32)).astype(BF16)

    across = lax.broadcasted_iota(jnp.int32, (group_rows, cap), 1).astype(F32)
    down = lax.broadcasted_iota(jnp.int32, (group_rows, cap), 0).astype(F32)
    mine = across == local_column
    position = jnp.sum(jnp.where(mine, down, 0.0), axis=0, keepdims=True)
    start = jnp.sum(jnp.where(mine, start_column, 0.0), axis=0, keepdims=True)
    stacked = per_shared * cap
    position = jnp.concatenate([position] * per_shared, axis=1)
    start = jnp.concatenate([start] * per_shared, axis=1)

    score_scale = 1.0 / math.sqrt(HEAD_SIZE)
    exp_scale = score_scale * math.log2(math.e)
    width = next((w for w in (256, 128) if stacked % w == 0), stacked)
    key_row = lax.broadcasted_iota(jnp.int32, (group_rows, width), 0).astype(F32)
    columns = [slice(i * HEAD_SIZE, (i + 1) * HEAD_SIZE) for i in range(per_shared)]
    queries = jnp.concatenate([query_ref[:, c] for c in columns], axis=0)
    grads = jnp.concatenate([grad_out[:, c] for c in columns], axis=0)
    probs_parts, score_parts = [], []
    for at in range(0, stacked, width):
        scores = matmul(key_block, queries[at : at + width], ROWS_ROWS)
        allowed = (key_row >= start[:, at : at + width]) & (key_row <= position[:, at : at + width])
        scores = jnp.where(allowed, scores, -1e30)
        highest = jnp.max(scores, axis=0, keepdims=True)
        lifted = jnp.exp2((scores - highest) * exp_scale)
        probs = lifted * (1.0 / jnp.sum(lifted, axis=0, keepdims=True))
        probs_low = probs.astype(BF16)
        grad_probs = matmul(value_block, grads[at : at + width], ROWS_ROWS)
        row_dot = jnp.sum(probs_low.astype(F32) * grad_probs, axis=0, keepdims=True)
        probs_parts.append(probs_low)
        score_parts.append((probs * ((grad_probs - row_dot) * score_scale)).astype(BF16))
    grad_scores = jnp.concatenate(score_parts, axis=1)
    head_query = matmul(grad_scores, key_block, COLS_COLS).astype(BF16)
    query_slots[pl.ds(pl.multiple_of(owner * cap, 16), cap), :] = jnp.concatenate(
        [head_query[i * cap : (i + 1) * cap] for i in range(per_shared)], axis=1
    )
    grad_key = matmul(grad_scores, queries)
    grad_value = matmul(jnp.concatenate(probs_parts, axis=1), grads)
    grad_own = jnp.concatenate([grad_key, grad_value], axis=1).astype(BF16)
    slot_down = lax.broadcasted_iota(jnp.int32, (slot_count, group_rows), 0).astype(F32)
    slot_to_row = jnp.where(slot_down == recv_row, 1.0, 0.0).astype(BF16)
    grad_back = matmul(slot_to_row, grad_own).astype(BF16)
    for source in range(owners):
        grad_slots[shared, source, pl.ds(pl.multiple_of(owner * cap, 16), cap), :] = grad_back[
            source * cap : (source + 1) * cap
        ]

    @pl.when(owner == owners - 1)
    def _():
        row = lax.broadcasted_iota(jnp.int32, (group_rows, slot_count), 0).astype(F32)
        spread = jnp.where(row == send_row_ref[0:1, :], 1.0, 0.0).astype(BF16)
        query_rows[shared] = matmul(spread, query_slots[...]).astype(BF16)
        for copy in exchange(0, shared):
            copy.start()

    @pl.when((shared == kv_here - 1) & (owner == owners - 1))
    def _():
        ring_first(kv_here - 1)

        def one_step(step, carry):
            ring_middle(kv_here - 1, step)
            return carry

        lax.fori_loop(1, owners - 1, one_step, 0)
        ring_last(kv_here - 1)

        def drain(step, carry):
            for which in range(kv_here):
                for way, chunk in every:
                    hop(which, way, step, chunk).wait_send()
            return carry

        lax.fori_loop(0, owners - 1, drain, 0)
        for which in range(kv_here):
            for item in range(3):
                for copy in exchange(item, which):
                    copy.wait()


def grads(owners, heads, cap, per_shared, row_info, send_row, query, upstream, kv_slots, send_all):
    slot_count = owners * cap
    kv_here = kv_slots.shape[-1] // HEAD_SIZE // 2
    wide = per_shared * HEAD_SIZE
    group_rows = row_info.shape[2]
    tok = group_rows // heads
    dma = pltpu.SemaphoreType.DMA
    anywhere = pl.BlockSpec(memory_space=pl.ANY)
    vmem = pl.BlockSpec(memory_space=pltpu.VMEM)
    rows_spec = pl.BlockSpec((cap, wide), lambda g, i: (i, g))

    def kv_spec(shift):
        return pl.BlockSpec((owners, None, cap, HEAD_SIZE), lambda g, i: (0, i, 0, g + shift))

    return pl.pallas_call(
        functools.partial(grads_kernel, owners, heads, cap, per_shared),
        grid=(kv_here, owners),
        in_specs=[
            pl.BlockSpec((1,) + row_info.shape[1:], lambda g, i: (i, 0, 0)),
            vmem,
            rows_spec,
            rows_spec,
            kv_spec(0),
            kv_spec(kv_here),
            vmem,
        ],
        out_specs=[anywhere] * 3,
        out_shape=[
            jax.ShapeDtypeStruct((tok, kv_here * wide * heads), BF16),
            jax.ShapeDtypeStruct((tok, kv_here * HEAD_SIZE * heads), BF16),
            jax.ShapeDtypeStruct((tok, kv_here * HEAD_SIZE * heads), BF16),
        ],
        scratch_shapes=[
            pltpu.VMEM((slot_count, wide), BF16),
            pltpu.VMEM((kv_here, group_rows, wide), BF16),
            pltpu.VMEM((kv_here, owners, slot_count, 2 * HEAD_SIZE), BF16),
            pltpu.VMEM((kv_here, 2, owners, 2, group_rows // 2, HEAD_SIZE), BF16),
            pltpu.VMEM((kv_here, 2, group_rows, HEAD_SIZE), BF16),
            dma((kv_here, 3)),
            dma((kv_here, 3, heads - 1)),
            dma((kv_here, 3, heads - 1)),
            dma((kv_here, 2, owners - 1, 2)),
            dma((kv_here, 2, owners - 1, 2)),
        ],
        compiler_params=pltpu.CompilerParams(
            collective_id=1, has_side_effects=True, vmem_limit_bytes=VMEM_BYTES
        ),
        name="attention_grads",
    )(row_info, send_row, query, upstream, kv_slots, kv_slots, send_all)


def pair_coefficients(doc_gap, pair_docs):
    docs = jnp.arange(doc_gap.shape[0], dtype=jnp.int32)
    chosen = pair_docs[0::2][:, None] == docs[None, :]
    rejected = pair_docs[1::2][:, None] == docs[None, :]
    sign = chosen.astype(F32) - rejected.astype(F32)
    margin = DPO_BETA * jnp.sum(sign * doc_gap[None, :], axis=1)
    weight = DPO_BETA * jax.nn.sigmoid(-margin)
    return -jnp.sum(sign * weight[:, None], axis=0)


def body(
    queries,
    keys,
    values,
    upstream,
    send_rows,
    recv_rows,
    doc_lengths,
    pair_docs,
    response_mask,
    policy_logp,
    ref_logp,
):
    tok_rows = queries.shape[0]
    head_devices = lax.axis_size("head")
    owners = lax.axis_size("seq")
    group_rows = tok_rows * head_devices
    slot_count = send_rows.shape[1]
    cap = slot_count // owners
    per_shared = queries.shape[1] // keys.shape[1]

    doc_len = doc_lengths[0]
    doc_count = doc_len.shape[0]
    doc_ends = jnp.cumsum(doc_len)
    position = jnp.arange(group_rows, dtype=jnp.int32)
    doc_of_row = jnp.sum((position[:, None] >= doc_ends[None, :]).astype(jnp.int32), axis=1)
    member = doc_of_row[:, None] == jnp.arange(doc_count, dtype=jnp.int32)[None, :]
    token_gap = response_mask.astype(F32) * (policy_logp - ref_logp)
    doc_gap = jnp.sum(jnp.where(member, token_gap[:, None], 0.0), axis=0)
    facts = jnp.concatenate(
        [send_rows[0].astype(F32), recv_rows[0].astype(F32), doc_len.astype(F32), doc_gap]
    )
    facts = jnp.pad(facts, (0, -facts.shape[0] % 128))
    facts = jnp.broadcast_to(facts[None, :], (8, facts.shape[0]))
    query_slots, upstream_slots, kv_slots, facts = gather(
        owners, head_devices, slot_count, queries, upstream, keys, values, facts
    )
    facts = facts[:, 0]

    send_all = facts[:, :slot_count]
    recv_all = facts[:, slot_count : slot_count + group_rows]
    at = slot_count + group_rows
    len_all = facts[:, at : at + doc_count]
    gap_all = facts[:, at + doc_count : at + 2 * doc_count]
    doc_coef = pair_coefficients(gap_all.reshape(-1), pair_docs).reshape(owners, doc_count)
    ends = jnp.cumsum(len_all, axis=1)
    starts = ends - len_all
    place = jnp.arange(group_rows, dtype=jnp.int32).astype(F32)
    inside = (place[None, :, None] >= starts[:, None, :]) & (place[None, :, None] < ends[:, None, :])
    start_of_row = jnp.sum(jnp.where(inside, starts[:, None, :], 0.0), axis=2)
    coef_of_row = jnp.sum(jnp.where(inside, doc_coef[:, None, :], 0.0), axis=2)
    first_slot = (lax.axis_index("seq") * cap).astype(F32)
    zero = jnp.zeros_like(recv_all)
    row_info = jnp.stack(
        [recv_all, recv_all - first_slot, start_of_row, coef_of_row, zero, zero, zero, zero], axis=1
    )
    own_send = send_rows[0].astype(F32)
    send_row = jnp.broadcast_to(own_send[None, :], (8, slot_count))

    kv_slots = kv_slots.reshape(owners, owners, cap, -1)
    return tuple(
        grads(
            owners,
            head_devices,
            cap,
            per_shared,
            row_info,
            send_row,
            query_slots,
            upstream_slots,
            kv_slots,
            send_all[:, None, :],
        )
    )


def solution(mesh):
    rows = P(("seq", "head"), None)
    return jax.shard_map(
        body,
        mesh=mesh,
        in_specs=(
            rows,
            rows,
            rows,
            rows,
            P("seq", None),
            P("seq", None),
            P("seq", None),
            P(),
            P("seq"),
            P("seq"),
            P("seq"),
        ),
        out_specs=(rows, rows, rows),
        check_vma=False,
    )
```
